256 devices in a mesh: dp: 64 (over x, z_lo, y, core), mp: 4 (over z_hi).
Axes of the slice: x: 4, y: 4, z: 8 (z_hi: 4, z_lo: 2; z = z_hi * 2 + z_lo), core: 2. Of those that a mesh axis runs over, the one named last changes fastest.
Arguments:
- query: bfloat16 [16384, 2560], P('dp', 'mp'), may hold values from -6 to 6
- key: bfloat16 [16384, 2560], P('dp', 'mp'), may hold values from -6 to 6
- value: bfloat16 [16384, 2560], P('dp', 'mp'), may hold values from -6 to 6
- residual: bfloat16 [16384, 5120], P(('dp', 'mp')), may hold values from -6 to 6
- cotangent: bfloat16 [16384, 5120], P(('dp', 'mp')), may hold values from -48 to 48
- out_weight: bfloat16 [5120, 2560], P('dp', 'mp'), may hold values from -1 to 1
- norm_gain: float32 [5120], replicated, may hold values from 0.1 to 1.9
- doc_ids: int32 [16384], P('dp'), may hold values from 0 to 1, as said below
Outputs:
- grad_query: bfloat16 [16384, 2560], P('dp', 'mp')
- grad_key: bfloat16 [16384, 2560], P('dp', 'mp')
- grad_value: bfloat16 [16384, 2560], P('dp', 'mp')
- grad_residual: bfloat16 [16384, 5120], P(('dp', 'mp'))
- grad_out_weight: float32 [5120, 2560], P('dp', 'mp')
- grad_gain: float32 [5120], P('dp')
The draws below stay inside these ranges and needn't reach their ends.
Inputs may be any that keep to these rules, and one draw needn't show every extreme that they name: `doc_ids`: within each sequence of 256 tokens the document numbers start at 0, never fall and rise by one at each new document; every sequence holds exactly 2 documents, each starting at a position that is a multiple of 8 within its sequence.
All inputs are finite; a program needn't handle non-finite values.
Results may differ from the reference program's by a relative error of at most 0.023.
Values may be sent and summed in bfloat16 or wider, within the bound.
No kernel may reach another device: no remote copies, remote signals or barrier semaphores. Data moves between devices by JAX's collectives and lax.ppermute only.
A program may use at most 128 MiB of HBM per device.

```python
import math
import jax
import jax.numpy as jnp
from jax import lax

D = 5120
HEADS = 20
HD = 128
SEQ = 256
DOCS = 2
TOKENS = 16384
N_DP = 64
N_MP = 4


def draw_query(key, part):
    key = jax.random.fold_in(key, 11)
    base = jnp.clip(jax.random.normal(key, (TOKENS, HEADS * HD), jnp.float32), -6.0, 6.0)
    return base.astype(jnp.bfloat16)


def draw_key(key, part):
    key = jax.random.fold_in(key, 12)
    base = jnp.clip(jax.random.normal(key, (TOKENS, HEADS * HD), jnp.float32), -6.0, 6.0)
    return base.astype(jnp.bfloat16)


def draw_value(key, part):
    key = jax.random.fold_in(key, 41)
    first, second = jax.random.split(key)
    group = HEADS * HD // N_MP
    common = jnp.clip(jax.random.normal(first, (TOKENS, group), jnp.float32), -4.5, 4.5)
    own = jnp.clip(jax.random.normal(second, (TOKENS, HEADS * HD), jnp.float32), -4.5, 4.5)
    base = 0.95 * jnp.tile(common, (1, N_MP)) + 0.35 * own
    return jnp.clip(base, -6.0, 6.0).astype(jnp.bfloat16)


def draw_out_weight(key, part):
    key = jax.random.fold_in(key, 51)
    first, second = jax.random.split(key)
    group = HEADS * HD // N_MP
    factor = 1.0 / math.sqrt(1.09 * HEADS * HD)
    common = jnp.clip(jax.random.normal(first, (D, group), jnp.float32), -5.0, 5.0)
    own = jnp.clip(jax.random.normal(second, (D, HEADS * HD), jnp.float32), -5.0, 5.0)
    base = (jnp.tile(common, (1, N_MP)) + 0.3 * own) * factor
    return jnp.clip(base, -1.0, 1.0).astype(jnp.bfloat16)


def draw_residual(key, part):
    key = jax.random.fold_in(key, 21)
    first, second, third = jax.random.split(key, 3)
    cols = jnp.exp(jax.random.uniform(second, (1, D), jnp.float32, math.log(0.3), math.log(3.0)))
    rows = jnp.exp(jax.random.uniform(first, (TOKENS, 1), jnp.float32, math.log(0.05), math.log(0.5)))
    base = jnp.clip(jax.random.normal(third, (TOKENS, D), jnp.float32), -4.0, 4.0) * rows * cols
    return jnp.clip(base, -6.0, 6.0).astype(jnp.bfloat16)


def draw_cotangent(key, part):
    key = jax.random.fold_in(key, 31)
    first, second = jax.random.split(key, 2)
    along = jnp.arange(TOKENS, dtype=jnp.float32)[:, None] / TOKENS
    rise = 1.0 + 2.0 * along
    rows = jnp.exp(jax.random.uniform(first, (TOKENS, 1), jnp.float32, 0.0, math.log(4.0)))
    base = jnp.clip(jax.random.normal(second, (TOKENS, D), jnp.float32), -4.0, 4.0) * rows * rise
    return jnp.clip(base, -48.0, 48.0).astype(jnp.bfloat16)


def draw_doc_ids(key, part):
    key = jax.random.fold_in(key, 5)
    blocks = SEQ // 8
    count = DOCS
    seqs = TOKENS // SEQ
    keys = jax.random.split(key, seqs)
    order = jax.vmap(lambda k: jax.random.permutation(k, blocks - 1))(keys)
    later = order < count - 1
    starts = jnp.concatenate([jnp.ones((seqs, 1), dtype=bool), later], axis=1)
    numbers = jnp.cumsum(starts.astype(jnp.int32), axis=1) - 1
    return jnp.repeat(numbers, 8, axis=1).reshape(TOKENS).astype(jnp.int32)


def setup_inputs(seed: int = 0) -> dict:
    splits = jax.random.split(jax.random.key(seed), 9)
    return {
        "query": draw_query(jax.random.fold_in(splits[8], 71), 0),
        "key": draw_key(jax.random.fold_in(splits[8], 71), 0),
        "value": draw_value(jax.random.fold_in(splits[8], 71), 0),
        "residual": draw_residual(jax.random.fold_in(splits[8], 71), 0),
        "cotangent": draw_cotangent(jax.random.fold_in(splits[8], 71), 0),
        "out_weight": draw_out_weight(jax.random.fold_in(splits[8], 71), 0),
        "norm_gain": jnp.clip(1.0 + 0.18 * jax.random.normal(splits[6], (D,), jnp.float32), 0.1, 1.9),
        "doc_ids": draw_doc_ids(jax.random.fold_in(splits[8], 71), 0),
    }


def attention_probs(query3, key3, ids):
    scale = 1.0 / math.sqrt(HD)
    scores = jnp.einsum('thd,shd->hts', query3.astype(jnp.float32), key3.astype(jnp.float32)) * scale
    pos = jnp.arange(SEQ, dtype=jnp.int32)
    allowed = (pos[None, :] <= pos[:, None]) & (ids[None, :] == ids[:, None])
    scores = jnp.where(allowed[None], scores, -1e+30)
    top = lax.optimization_barrier(jnp.max(scores, axis=2, keepdims=True))
    weights = jnp.exp(scores - top)
    return weights / lax.optimization_barrier(jnp.sum(weights, axis=2, keepdims=True))

def reference(query, key, value, residual, cotangent, out_weight, norm_gain, doc_ids):
    local = HEADS // N_MP * HD
    scale = 1.0 / math.sqrt(HD)
    width = HEADS * HD

    def one(carry, items):
        grad_w, grad_g = carry
        q_rows, k_rows, v_rows, x_rows, cot_rows, ids = items
        query3 = q_rows.reshape(SEQ, HEADS, HD)
        key3 = k_rows.reshape(SEQ, HEADS, HD)
        value3 = v_rows.reshape(SEQ, HEADS, HD)
        probs = attention_probs(query3, key3, ids)
        probs_b = probs.astype(jnp.bfloat16)
        attended = jnp.einsum('hts,shd->thd', probs_b.astype(jnp.float32), value3.astype(jnp.float32))
        attended = attended.astype(jnp.bfloat16).reshape(SEQ, width)
        branch = jnp.zeros((SEQ, D), jnp.float32)
        for group in range(N_MP):
            part = jnp.dot(attended[:, group * local:(group + 1) * local], out_weight[:, group * local:(group + 1) * local].T, preferred_element_type=jnp.float32)
            branch = branch + lax.optimization_barrier(part.astype(jnp.bfloat16)).astype(jnp.float32)
        mixed = x_rows.astype(jnp.float32) + branch
        inv = lax.rsqrt(lax.optimization_barrier(jnp.mean(mixed * mixed, axis=1, keepdims=True)) + 1e-05)
        gscaled = cot_rows.astype(jnp.float32) * norm_gain.astype(jnp.float32)
        grad_h = inv * (gscaled - mixed * inv * inv * lax.optimization_barrier(jnp.mean(gscaled * mixed, axis=1, keepdims=True)))
        grad_res = grad_h.astype(jnp.bfloat16)
        grad_g = grad_g + lax.optimization_barrier(jnp.sum(cot_rows.astype(jnp.float32) * mixed * inv, axis=0))
        grad_w = grad_w + lax.dot_general(grad_res, attended, (((0,), (0,)), ((), ())), preferred_element_type=jnp.float32)
        grad_att = jnp.dot(grad_res, out_weight, preferred_element_type=jnp.float32).astype(jnp.bfloat16)
        grad3 = grad_att.reshape(SEQ, HEADS, HD).astype(jnp.float32)
        grad_v = jnp.einsum('hts,thd->shd', probs_b.astype(jnp.float32), grad3).astype(jnp.bfloat16)
        grad_probs = jnp.einsum('thd,shd->hts', grad3, value3.astype(jnp.float32))
        delta = lax.optimization_barrier(jnp.sum(probs * grad_probs, axis=2, keepdims=True))
        grad_scores = (probs * (grad_probs - delta)).astype(jnp.bfloat16).astype(jnp.float32)
        grad_q = (jnp.einsum('hts,shd->thd', grad_scores, key3.astype(jnp.float32)) * scale).astype(jnp.bfloat16)
        grad_k = (jnp.einsum('hts,thd->shd', grad_scores, query3.astype(jnp.float32)) * scale).astype(jnp.bfloat16)
        outs = (grad_q.reshape(SEQ, width), grad_k.reshape(SEQ, width), grad_v.reshape(SEQ, width), grad_res)
        return ((grad_w, grad_g), outs)
    items = (query.reshape(N_DP, SEQ, width), key.reshape(N_DP, SEQ, width), value.reshape(N_DP, SEQ, width), residual.reshape(N_DP, SEQ, D), cotangent.reshape(N_DP, SEQ, D), doc_ids.reshape(N_DP, SEQ))
    start = (jnp.zeros((D, width), jnp.float32), jnp.zeros((D,), jnp.float32))
    (grad_w, grad_g), outs = lax.scan(one, start, items)
    grad_query = outs[0].reshape(TOKENS, width)
    grad_key = outs[1].reshape(TOKENS, width)
    grad_value = outs[2].reshape(TOKENS, width)
    grad_residual = outs[3].reshape(TOKENS, D)
    return (grad_query, grad_key, grad_value, grad_residual, grad_w / N_DP, grad_g / N_DP)
```

```python
import math

import jax
import jax.numpy as jnp
from jax import lax
from jax.experimental import pallas as pl
from jax.experimental.pallas import tpu as pltpu
from jax.sharding import PartitionSpec as P

HD = 128
BF = jnp.bfloat16
F32 = jnp.float32
GROUPS = ((0,), (1,), (2,), (3,))
VMEM_LIMIT = 40 * 1024 * 1024


def dp_perm(dx=0, dy=0, flip_w=False, flip_c=False):
    pairs = []
    for i in range(64):
        c, y, w, x = i % 2, i // 2 % 4, i // 8 % 2, i // 16
        w, c = w ^ flip_w, c ^ flip_c
        x, y = (x + dx) % 4, (y + dy) % 4
        pairs.append((i, ((x * 2 + w) * 4 + y) * 2 + c))
    return pairs


def send_dp(value, **step):
    return lax.ppermute(value, "dp", dp_perm(**step))


def send_mp(value, step):
    return lax.ppermute(value, "mp", [(i, (i + step) % 4) for i in range(4)])


def attention_probs(query3, key3, doc_ids):
    seq = query3.shape[0]
    scale = 1.0 / math.sqrt(HD)
    scores = jnp.einsum("thd,shd->hts", query3, key3, preferred_element_type=F32) * scale
    pos = lax.iota(jnp.int32, seq)
    allowed = (pos[None, :] <= pos[:, None]) & (doc_ids[None, :] == doc_ids[:, None])
    scores = jnp.where(allowed[None], scores, -1e30)
    top = jnp.max(scores, axis=2, keepdims=True)
    weights = jnp.exp(scores - top)
    return weights / jnp.sum(weights, axis=2, keepdims=True)


def turn_tokens(pos, att_ref, att_s):
    rows = att_ref.shape[0] // 4
    for k in range(4):
        start = pl.multiple_of(((pos[2] + k) % 4) * rows, 16)
        att_s[pl.ds(k * rows, rows), :] = att_ref[pl.ds(start, rows), :]


def branch_kernel(pos, att_ref, cat_ref, oth_ref, w_ref, p0, p1, p2a, p2b, p3, att_s):
    _, nj, _, piece, _ = cat_ref.shape
    y, c = pos[0], pos[1]
    turn_tokens(pos, att_ref, att_s)
    rows = att_ref.shape[0] // 4
    half = rows // 2
    span = 16 * piece
    for j in range(nj):
        for w in range(2):
            for k in range(4):
                base = ((j * 2 + w) * 4 + (y + k) % 4) * 2
                mine = pl.multiple_of((base + c) * piece, 16)
                other = pl.multiple_of((base + 1 - c) * piece, 16)
                w_ref[pl.ds(mine, piece), :] = cat_ref[k, j, w]
                w_ref[pl.ds(other, piece), :] = oth_ref[k, j, w]
        cols = pl.ds(j * span, span)
        prod = lax.dot_general(
            att_s[...], w_ref[cols, :], (((1,), (1,)), ((), ())), preferred_element_type=F32
        ).astype(BF)
        p0[:, cols] = prod[:rows]
        p1[:, cols] = prod[rows : 2 * rows]
        p2a[:, cols] = prod[2 * rows : 2 * rows + half]
        p2b[:, cols] = prod[2 * rows + half : 3 * rows]
        p3[:, cols] = prod[3 * rows :]


def branch_part(pos, attended, cat, oth):
    _, nj, _, piece, width = cat.shape
    seq = attended.shape[0]
    rows, span = seq // 4, nj * 16 * piece
    sds = jax.ShapeDtypeStruct
    vm = pl.BlockSpec(memory_space=pltpu.VMEM)
    return pl.pallas_call(
        branch_kernel,
        in_specs=[pl.BlockSpec(memory_space=pltpu.SMEM), vm, vm, vm],
        out_specs=[vm] * 6,
        out_shape=[
            sds((span, width), BF),
            sds((rows, span), BF),
            sds((rows, span), BF),
            sds((rows // 2, span), BF),
            sds((rows // 2, span), BF),
            sds((rows, span), BF),
        ],
        scratch_shapes=[pltpu.VMEM((seq, width), BF)],
        compiler_params=pltpu.CompilerParams(vmem_limit_bytes=VMEM_LIMIT),
        cost_estimate=pl.CostEstimate(
            flops=2 * seq * width * span,
            bytes_accessed=2 * (3 * span * width + seq * span),
            transcendentals=0,
        ),
        name="branch_part",
    )(pos, attended, cat, oth)


def grads_kernel(pos, g0, gp, ga, gb, gm, att_ref, w_ref, acc_ref, keep, send, acc_out, att_s, rows_s):
    _, nj, _, piece, _ = keep.shape
    y, c = pos[0], pos[1]
    turn_tokens(pos, att_ref, att_s)
    rows = g0.shape[0]
    half = rows // 2
    span = 16 * piece
    rows_s[pl.ds(0, rows), :] = g0[...]
    rows_s[pl.ds(rows, rows), :] = gp[...]
    rows_s[pl.ds(2 * rows, half), :] = ga[...]
    rows_s[pl.ds(2 * rows + half, half), :] = gb[...]
    rows_s[pl.ds(3 * rows, rows), :] = gm[...]
    acc = acc_ref[...]
    for j in range(nj):
        cols = pl.ds(j * span, span)
        acc = acc + jnp.dot(rows_s[:, cols], w_ref[cols, :], preferred_element_type=F32)
        prod = lax.dot_general(
            rows_s[:, cols], att_s[...], (((0,), (0,)), ((), ())), preferred_element_type=F32
        ).astype(BF)
        for w in range(2):
            for q in range(4):
                k = (q - y + 4) % 4
                base = (w * 4 + q) * 2
                even = prod[base * piece : (base + 1) * piece]
                odd = prod[(base + 1) * piece : (base + 2) * piece]
                keep[k, j, w] = jnp.where(c == 0, even, odd)
                send[k, j, w] = jnp.where(c == 0, odd, even)
    acc_out[...] = acc


def grads_part(nj, pos, g0, gp, ga, gb, gm, attended, weight, acc):
    span, width = weight.shape
    seq = attended.shape[0]
    piece = span // (16 * nj)
    sds = jax.ShapeDtypeStruct
    vm = pl.BlockSpec(memory_space=pltpu.VMEM)
    return pl.pallas_call(
        grads_kernel,
        in_specs=[pl.BlockSpec(memory_space=pltpu.SMEM)] + [vm] * 8,
        out_specs=[vm] * 3,
        out_shape=[
            sds((4, nj, 2, piece, width), BF),
            sds((4, nj, 2, piece, width), BF),
            sds((seq, width), F32),
        ],
        scratch_shapes=[pltpu.VMEM((seq, width), BF), pltpu.VMEM((seq, span), BF)],
        compiler_params=pltpu.CompilerParams(vmem_limit_bytes=VMEM_LIMIT),
        cost_estimate=pl.CostEstimate(
            flops=4 * seq * width * span,
            bytes_accessed=2 * (2 * span * width + seq * span),
            transcendentals=0,
        ),
        name="grads_part",
    )(pos, g0, gp, ga, gb, gm, attended, weight, acc)


def sum_f32(*parts):
    total = parts[0].astype(F32)
    for part in parts[1:]:
        total = total + part.astype(F32)
    return total


def on_device(query, key, value, residual, cotangent, out_weight, norm_gain, doc_ids):
    seq, width = query.shape
    heads = width // HD
    piece = out_weight.shape[0]
    rows, d_model = residual.shape
    half = rows // 2
    span = d_model // 4
    scale = 1.0 / math.sqrt(HD)
    dp = lax.axis_index("dp")
    m = lax.axis_index("mp")
    x, w, y, c = dp // 16, dp // 8 % 2, dp // 2 % 4, dp % 2
    pos = jnp.stack([y, c, m]).astype(jnp.int32)

    across = send_dp(out_weight, flip_w=True)
    pair = jnp.where(w == 0, jnp.stack([out_weight, across]), jnp.stack([across, out_weight]))
    planes = [pair] + [send_dp(pair, dx=-j) for j in (1, 2, 3)]

    query3 = query.reshape(seq, heads, HD)
    key3 = key.reshape(seq, heads, HD)
    value3 = value.reshape(seq, heads, HD)
    probs = attention_probs(query3, key3, doc_ids)
    probs_b = probs.astype(BF)
    attended = jnp.einsum("hts,shd->thd", probs_b, value3, preferred_element_type=F32)
    attended = attended.astype(BF).reshape(seq, width)

    def plane_cols(array, j):
        return lax.dynamic_slice_in_dim(array, ((x + j) % 4) * span, span, array.ndim - 1)

    weights, mixed, gscaled, cot = [], [], [], []
    sq = jnp.zeros((rows, 1), F32)
    dot = jnp.zeros((rows, 1), F32)
    for group in GROUPS:
        mine = jnp.stack([planes[j] for j in group])
        cat = jnp.stack([mine] + [send_dp(mine, dy=-k) for k in (1, 2, 3)])
        oth = send_dp(cat, flip_c=True)
        weight, p0, p1, p2a, p2b, p3 = branch_part(pos, attended, cat, oth)
        weights.append(weight)
        ra = send_mp(p2a, 1)
        rb = send_mp(p2b, -1)
        up = jnp.concatenate([sum_f32(p1[:half], ra).astype(BF), p1[half:]])
        down = jnp.concatenate([p3[:half], sum_f32(p3[half:], rb).astype(BF)])
        branch = sum_f32(p0, send_mp(up, 1), send_mp(down, -1))
        res = jnp.concatenate([plane_cols(residual, j) for j in group], 1).astype(F32)
        ct = jnp.concatenate([plane_cols(cotangent, j) for j in group], 1).astype(F32)
        gain = jnp.concatenate([plane_cols(norm_gain, j) for j in group])
        mx = res + branch
        gs = ct * gain
        sq = sq + jnp.sum(mx * mx, axis=1, keepdims=True)
        dot = dot + jnp.sum(gs * mx, axis=1, keepdims=True)
        mixed.append(mx)
        gscaled.append(gs)
        cot.append(ct)

    inv = lax.rsqrt(sq / d_model + 1e-05)
    mean_dot = dot / d_model

    grad_residual = jnp.zeros((rows, d_model), BF)
    gain_rows = jnp.zeros((4, span), F32)
    acc = jnp.zeros((seq, width), F32)
    outgoing = {}
    for index, group in enumerate(GROUPS):
        mx, gs, ct = mixed[index], gscaled[index], cot[index]
        g0 = (inv * (gs - mx * inv * inv * mean_dot)).astype(BF)
        stat = jnp.sum(ct * mx * inv, axis=0)
        for n, j in enumerate(group):
            at = (x + j) % 4
            grad_residual = lax.dynamic_update_slice_in_dim(
                grad_residual, g0[:, n * span : (n + 1) * span], at * span, 1
            )
            gain_rows = lax.dynamic_update_slice_in_dim(
                gain_rows, stat[None, n * span : (n + 1) * span], at, 0
            )
        gm = send_mp(g0, 1)
        gp = send_mp(g0, -1)
        ga = send_mp(gm[:half], 1)
        gb = send_mp(gp[half:], -1)
        keep, send, acc = grads_part(
            len(group), pos, g0, gp, ga, gb, gm, attended, weights[index], acc
        )
        got = send_dp(send, flip_c=True)
        both = sum_f32(keep, got).astype(BF)
        part = sum_f32(both[0], *[send_dp(both[k], dy=k) for k in (1, 2, 3)]).astype(BF)
        for n, j in enumerate(group):
            outgoing[j] = part[n]

    total = sum_f32(outgoing[0], *[send_dp(outgoing[j], dx=j) for j in (1, 2, 3)])
    home = jnp.where(w == 0, total[0], total[1])
    away = jnp.where(w == 0, total[1], total[0]).astype(BF)
    grad_weight = (home + send_dp(away, flip_w=True).astype(F32)) / 64

    gain_total = gain_rows.reshape(d_model // 128, 128)
    gain_total = gain_total + lax.ppermute(gain_total, "mp", [(i, i ^ 1) for i in range(4)])
    gain_total = gain_total + lax.ppermute(gain_total, "mp", [(i, i ^ 2) for i in range(4)])
    for bit in (1, 8, 2, 4, 16, 32):
        gain_total = gain_total + lax.ppermute(gain_total, "dp", [(i, i ^ bit) for i in range(64)])
    grad_gain = lax.dynamic_slice_in_dim(gain_total.reshape(d_model) / 64, dp * piece, piece, 0)

    acc = jnp.concatenate([acc, acc])
    grad_attended = lax.dynamic_slice_in_dim(acc, ((4 - m) % 4) * rows, seq, 0).astype(BF)
    grad3 = grad_attended.reshape(seq, heads, HD)
    grad_value = jnp.einsum("hts,thd->shd", probs_b, grad3, preferred_element_type=F32)
    grad_value = grad_value.astype(BF).reshape(seq, width)
    grad_probs = jnp.einsum("thd,shd->hts", grad3, value3, preferred_element_type=F32)
    delta = jnp.sum(probs * grad_probs, axis=2, keepdims=True)
    grad_scores = (probs * (grad_probs - delta)).astype(BF)
    grad_query = jnp.einsum("hts,shd->thd", grad_scores, key3, preferred_element_type=F32) * scale
    grad_key = jnp.einsum("hts,thd->shd", grad_scores, query3, preferred_element_type=F32) * scale
    grad_query = grad_query.astype(BF).reshape(seq, width)
    grad_key = grad_key.astype(BF).reshape(seq, width)
    return (grad_query, grad_key, grad_value, grad_residual, grad_weight, grad_gain)


def solution(mesh):
    placed = (
        P("dp", "mp"),
        P("dp", "mp"),
        P("dp", "mp"),
        P(("dp", "mp"), None),
        P(("dp", "mp"), None),
        P("dp", "mp"),
        P(),
        P("dp"),
    )
    return jax.shard_map(
        on_device,
        mesh=mesh,
        in_specs=placed,
        out_specs=(
            P("dp", "mp"),
            P("dp", "mp"),
            P("dp", "mp"),
            P(("dp", "mp"), None),
            P("dp", "mp"),
            P("dp"),
        ),
        check_vma=False,
    )
```

```python
import math

import jax
import jax.numpy as jnp
from jax import lax
from jax.experimental import pallas as pl
from jax.experimental.pallas import tpu as pltpu
from jax.sharding import PartitionSpec as P

HD = 128
BF = jnp.bfloat16
F32 = jnp.float32
VMEM_LIMIT = 40 * 1024 * 1024


CHIPS = [[2 * i + c for i in range(32)] for c in range(2)]
FLIP_C = [(i, i ^ 1) for i in range(64)]


def swap(value, pairs):
    return lax.ppermute(value, "dp", pairs)


def send_mp(value, step):
    return lax.ppermute(value, "mp", [(i, (i + step) % 4) for i in range(4)])


def exchange(blocks, groups):
    return lax.all_to_all(blocks, "dp", 0, 0, axis_index_groups=groups)


def spread(block):
    return jnp.broadcast_to(block[None], (4, *block.shape))


def attention_probs(query3, key3, doc_ids):
    seq = query3.shape[0]
    scale = 1.0 / math.sqrt(HD)
    scores = jnp.einsum("thd,shd->hts", query3, key3, preferred_element_type=F32) * scale
    pos = lax.iota(jnp.int32, seq)
    allowed = (pos[None, :] <= pos[:, None]) & (doc_ids[None, :] == doc_ids[:, None])
    scores = jnp.where(allowed[None], scores, -1e30)
    top = jnp.max(scores, axis=2, keepdims=True)
    weights = jnp.exp(scores - top)
    return weights / jnp.sum(weights, axis=2, keepdims=True)


def turn_tokens(pos, att_ref, att_s):
    rows = att_ref.shape[0] // 4
    for k in range(4):
        start = pl.multiple_of(((pos[1] + k) % 4) * rows, 16)
        att_s[pl.ds(k * rows, rows), :] = att_ref[pl.ds(start, rows), :]


def branch_kernel(pos, att_ref, cat_ref, oth_ref, w_ref, p0, p1a, p1b, p2a, p2b, p3a, p3b, att_s):
    count, piece, _ = cat_ref.shape
    c = pos[0]
    rows = att_ref.shape[0] // 4
    half = rows // 2

    @pl.when(pl.program_id(0) == 0)
    def _():
        turn_tokens(pos, att_ref, att_s)

    for i in range(count):
        mine = pl.multiple_of((2 * i + c) * piece, 16)
        other = pl.multiple_of((2 * i + 1 - c) * piece, 16)
        w_ref[pl.ds(mine, piece), :] = cat_ref[i]
        w_ref[pl.ds(other, piece), :] = oth_ref[i]
    prod = lax.dot_general(
        att_s[...], w_ref[...], (((1,), (1,)), ((), ())), preferred_element_type=F32
    ).astype(BF)
    p0[...] = prod[:rows]
    p1a[...] = prod[rows : rows + half]
    p1b[...] = prod[rows + half : 2 * rows]
    p2a[...] = prod[2 * rows : 2 * rows + half]
    p2b[...] = prod[2 * rows + half : 3 * rows]
    p3a[...] = prod[3 * rows : 3 * rows + half]
    p3b[...] = prod[3 * rows + half :]


def branch_part(pos, attended, cat, oth):
    count, piece, width = cat.shape
    seq = attended.shape[0]
    rows, span, total = seq // 4, 16 * piece, 2 * count * piece
    sds = jax.ShapeDtypeStruct
    heights = (rows,) + (rows // 2,) * 6
    block = pl.BlockSpec((8, piece, width), lambda i: (i, 0, 0))
    return pl.pallas_call(
        branch_kernel,
        grid=(count // 8,),
        in_specs=[
            pl.BlockSpec(memory_space=pltpu.SMEM),
            pl.BlockSpec((seq, width), lambda i: (0, 0)),
            block,
            block,
        ],
        out_specs=[pl.BlockSpec((span, width), lambda i: (i, 0))]
        + [pl.BlockSpec((h, span), lambda i: (0, i)) for h in heights],
        out_shape=[sds((total, width), BF)] + [sds((h, total), BF) for h in heights],
        scratch_shapes=[pltpu.VMEM((seq, width), BF)],
        compiler_params=pltpu.CompilerParams(vmem_limit_bytes=VMEM_LIMIT),
        cost_estimate=pl.CostEstimate(
            flops=2 * seq * width * total,
            bytes_accessed=2 * (2 * total * width + seq * total),
            transcendentals=0,
        ),
        name="branch_part",
    )(pos, attended, cat, oth)


def grads_kernel(
    pos, _, g0, gp, ga, gb, gm, att_ref, w_ref, keep, send, out_ref, att_s, rows_s, acc
):
    count, piece, _ = keep.shape
    c, m = pos[0], pos[1]
    rows = g0.shape[0]
    half = rows // 2
    step = pl.program_id(0)

    @pl.when(step == 0)
    def _():
        turn_tokens(pos, att_ref, att_s)
        acc[...] = jnp.zeros_like(acc)

    rows_s[pl.ds(0, rows), :] = g0[...]
    rows_s[pl.ds(rows, rows), :] = gp[...]
    rows_s[pl.ds(2 * rows, half), :] = ga[...]
    rows_s[pl.ds(2 * rows + half, half), :] = gb[...]
    rows_s[pl.ds(3 * rows, rows), :] = gm[...]
    acc[...] += jnp.dot(rows_s[...], w_ref[...], preferred_element_type=F32)
    prod = lax.dot_general(
        rows_s[...], att_s[...], (((0,), (0,)), ((), ())), preferred_element_type=F32
    ).astype(BF)
    for i in range(count):
        even = prod[2 * i * piece : (2 * i + 1) * piece]
        odd = prod[(2 * i + 1) * piece : (2 * i + 2) * piece]
        keep[i] = jnp.where(c == 0, even, odd)
        send[i] = jnp.where(c == 0, odd, even)

    @pl.when(step == pl.num_programs(0) - 1)
    def _():
        for k in range(4):
            start = pl.multiple_of(((m + k) % 4) * rows, 16)
            out_ref[pl.ds(start, rows), :] = acc[pl.ds(k * rows, rows), :].astype(BF)


def grads_part(pos, gain, g0, gp, ga, gb, gm, attended, weight, piece):
    total, width = weight.shape
    seq = attended.shape[0]
    count, span = total // (2 * piece), 16 * piece
    sds = jax.ShapeDtypeStruct
    whole = pl.BlockSpec((seq, width), lambda i: (0, 0))
    block = pl.BlockSpec((8, piece, width), lambda i: (i, 0, 0))
    return pl.pallas_call(
        grads_kernel,
        grid=(count // 8,),
        in_specs=[pl.BlockSpec(memory_space=pltpu.SMEM), pl.BlockSpec(memory_space=pl.ANY)]
        + [pl.BlockSpec((g.shape[0], span), lambda i: (0, i)) for g in (g0, gp, ga, gb, gm)]
        + [whole, pl.BlockSpec((span, width), lambda i: (i, 0))],
        out_specs=[block, block, whole],
        out_shape=[
            sds((count, piece, width), BF),
            sds((count, piece, width), BF),
            sds((seq, width), BF),
        ],
        scratch_shapes=[
            pltpu.VMEM((seq, width), BF),
            pltpu.VMEM((seq, span), BF),
            pltpu.VMEM((seq, width), F32),
        ],
        compiler_params=pltpu.CompilerParams(vmem_limit_bytes=VMEM_LIMIT),
        cost_estimate=pl.CostEstimate(
            flops=4 * seq * width * total,
            bytes_accessed=2 * (2 * total * width + seq * total),
            transcendentals=0,
        ),
        name="grads_part",
    )(pos, gain, g0, gp, ga, gb, gm, attended, weight)


def sum_f32(*parts):
    total = parts[0].astype(F32)
    for part in parts[1:]:
        total = total + part.astype(F32)
    return total


def on_device(query, key, value, residual, cotangent, out_weight, norm_gain, doc_ids):
    seq, width = query.shape
    heads = width // HD
    piece = out_weight.shape[0]
    rows, d_model = residual.shape
    half = rows // 2
    scale = 1.0 / math.sqrt(HD)
    dp = lax.axis_index("dp")
    c = dp % 2
    m = lax.axis_index("mp")
    pos = jnp.stack([c, m]).astype(jnp.int32)

    copies = jnp.broadcast_to(out_weight[None], (32, piece, width))
    cat = exchange(copies, CHIPS)

    query3 = query.reshape(seq, heads, HD)
    key3 = key.reshape(seq, heads, HD)
    value3 = value.reshape(seq, heads, HD)
    probs = attention_probs(query3, key3, doc_ids)
    probs_b = probs.astype(BF)
    attended = jnp.einsum("hts,shd->thd", probs_b, value3, preferred_element_type=F32)
    attended = attended.astype(BF).reshape(seq, width)

    cat, attended = lax.optimization_barrier((cat, attended))
    oth = swap(cat, FLIP_C)
    weight, p0, p1a, p1b, p2a, p2b, p3a, p3b = branch_part(pos, attended, cat, oth)
    ra = send_mp(p2a, 1)
    rb = send_mp(p2b, -1)
    up_b = send_mp(p1b, 1)
    down_a = send_mp(p3a, -1)
    up_a = send_mp(sum_f32(p1a, ra).astype(BF), 1)
    down_b = send_mp(sum_f32(p3b, rb).astype(BF), -1)
    up = jnp.concatenate([up_a, up_b])
    down = jnp.concatenate([down_a, down_b])
    mixed = sum_f32(residual, p0, up, down)
    cot = cotangent.astype(F32)
    gscaled = cot * norm_gain
    inv = lax.rsqrt(jnp.mean(mixed * mixed, axis=1, keepdims=True) + 1e-05)
    mean_dot = jnp.mean(gscaled * mixed, axis=1, keepdims=True)
    grad_residual = (inv * (gscaled - mixed * inv * inv * mean_dot)).astype(BF)

    gain_rows = jnp.sum(cot * mixed * inv, axis=0).reshape(64, 1, piece)
    gain_rows = jnp.sum(lax.all_to_all(gain_rows, "dp", 0, 0), axis=0)
    gm = send_mp(grad_residual, 1)
    gp = send_mp(grad_residual, -1)
    gm, gp, gain_rows = lax.optimization_barrier((gm, gp, gain_rows))
    ga = send_mp(gm[:half], 1)
    gb = send_mp(gp[half:], -1)
    gain_rows = lax.all_to_all(spread(gain_rows), "mp", 0, 0)
    grad_gain = jnp.sum(gain_rows, axis=0).reshape(piece) / 64
    keep, send, grad_attended = grads_part(
        pos, grad_gain, grad_residual, gp, ga, gb, gm, attended, weight, piece
    )
    both = sum_f32(keep, swap(send, FLIP_C)).astype(BF)
    grad_weight = jnp.sum(exchange(both, CHIPS).astype(F32), axis=0) / 64

    grad3 = grad_attended.reshape(seq, heads, HD)
    grad_value = jnp.einsum("hts,thd->shd", probs_b, grad3, preferred_element_type=F32)
    grad_value = grad_value.astype(BF).reshape(seq, width)
    grad_probs = jnp.einsum("thd,shd->hts", grad3, value3, preferred_element_type=F32)
    delta = jnp.sum(probs * grad_probs, axis=2, keepdims=True)
    grad_scores = (probs * (grad_probs - delta)).astype(BF)
    grad_query = jnp.einsum("hts,shd->thd", grad_scores, key3, preferred_element_type=F32) * scale
    grad_key = jnp.einsum("hts,thd->shd", grad_scores, query3, preferred_element_type=F32) * scale
    grad_query = grad_query.astype(BF).reshape(seq, width)
    grad_key = grad_key.astype(BF).reshape(seq, width)
    return (grad_query, grad_key, grad_value, grad_residual, grad_weight, grad_gain)


def solution(mesh):
    placed = (
        P("dp", "mp"),
        P("dp", "mp"),
        P("dp", "mp"),
        P(("dp", "mp"), None),
        P(("dp", "mp"), None),
        P("dp", "mp"),
        P(),
        P("dp"),
    )
    return jax.shard_map(
        on_device,
        mesh=mesh,
        in_specs=placed,
        out_specs=(
            P("dp", "mp"),
            P("dp", "mp"),
            P("dp", "mp"),
            P(("dp", "mp"), None),
            P("dp", "mp"),
            P("dp"),
        ),
        check_vma=False,
    )
```

```python
import math

import jax
import jax.numpy as jnp
from jax import lax
from jax.experimental import pallas as pl
from jax.experimental.pallas import tpu as pltpu
from jax.sharding import PartitionSpec as P

HD = 128
BF = jnp.bfloat16
F32 = jnp.float32
VMEM_LIMIT = 40 * 1024 * 1024


def rings(along_y):
    groups = []
    for c in range(2):
        for w in range(2):
            for line in range(4):
                places = [(line, k) if (c == 0) == along_y else (k, line) for k in range(4)]
                groups.append([((x * 2 + w) * 4 + y) * 2 + c for x, y in places])
    return groups


NEAR, FAR = rings(True), rings(False)
FLIP_W = [(i, i ^ 8) for i in range(64)]
FLIP_C = [(i, i ^ 1) for i in range(64)]


def swap(value, pairs):
    return lax.ppermute(value, "dp", pairs)


def send_mp(value, step):
    return lax.ppermute(value, "mp", [(i, (i + step) % 4) for i in range(4)])


def exchange(blocks, groups):
    return lax.all_to_all(blocks, "dp", 0, 0, axis_index_groups=groups)


def spread(block):
    return jnp.broadcast_to(block[None], (4, *block.shape))


def attention_probs(query3, key3, doc_ids):
    seq = query3.shape[0]
    scale = 1.0 / math.sqrt(HD)
    scores = jnp.einsum("thd,shd->hts", query3, key3, preferred_element_type=F32) * scale
    pos = lax.iota(jnp.int32, seq)
    allowed = (pos[None, :] <= pos[:, None]) & (doc_ids[None, :] == doc_ids[:, None])
    scores = jnp.where(allowed[None], scores, -1e30)
    top = jnp.max(scores, axis=2, keepdims=True)
    weights = jnp.exp(scores - top)
    return weights / jnp.sum(weights, axis=2, keepdims=True)


def turn_tokens(pos, att_ref, att_s):
    rows = att_ref.shape[0] // 4
    for k in range(4):
        start = pl.multiple_of(((pos[1] + k) % 4) * rows, 16)
        att_s[pl.ds(k * rows, rows), :] = att_ref[pl.ds(start, rows), :]


def place(c, x, y):
    return jnp.where(c == 0, x, y), jnp.where(c == 0, y, x)


def branch_kernel(pos, att_ref, *refs):
    mine, other = refs[:4], refs[4:8]
    w_ref, p0, p1a, p1b, p2a, p2b, p3a, p3b, att_s = refs[8:]
    piece = mine[0].shape[3]
    c = pos[0]
    rows = att_ref.shape[0] // 4
    half = rows // 2

    @pl.when(pl.program_id(0) == 0)
    def _():
        turn_tokens(pos, att_ref, att_s)

    for w in range(2):
        for y in range(4):
            i = w * 4 + y
            w_ref[pl.ds(pl.multiple_of((2 * i + c) * piece, 16), piece), :] = mine[y][0, 0, w]
            w_ref[pl.ds(pl.multiple_of((2 * i + 1 - c) * piece, 16), piece), :] = other[y][0, 0, w]
    prod = lax.dot_general(
        att_s[...], w_ref[...], (((1,), (1,)), ((), ())), preferred_element_type=F32
    ).astype(BF)
    p0[...] = prod[:rows]
    p1a[...] = prod[rows : rows + half]
    p1b[...] = prod[rows + half : 2 * rows]
    p2a[...] = prod[2 * rows : 2 * rows + half]
    p2b[...] = prod[2 * rows + half : 3 * rows]
    p3a[...] = prod[3 * rows : 3 * rows + half]
    p3b[...] = prod[3 * rows + half :]


def branch_part(pos, attended, cat, oth):
    piece, width = cat.shape[3:]
    seq = attended.shape[0]
    rows, span = seq // 4, 16 * piece
    total = 4 * span
    sds = jax.ShapeDtypeStruct
    heights = (rows,) + (rows // 2,) * 6

    def block(flip, y):
        def at(i, pos):
            return *place(pos[0] ^ flip, i, y), 0, 0, 0

        return pl.BlockSpec((1, 1, 2, piece, width), at)

    return pl.pallas_call(
        branch_kernel,
        grid_spec=pltpu.PrefetchScalarGridSpec(
            num_scalar_prefetch=1,
            grid=(4,),
            in_specs=[pl.BlockSpec((seq, width), lambda i, pos: (0, 0))]
            + [block(flip, y) for flip in range(2) for y in range(4)],
            out_specs=[pl.BlockSpec((span, width), lambda i, pos: (i, 0))]
            + [pl.BlockSpec((h, span), lambda i, pos: (0, i)) for h in heights],
            scratch_shapes=[pltpu.VMEM((seq, width), BF)],
        ),
        out_shape=[sds((total, width), BF)] + [sds((h, total), BF) for h in heights],
        compiler_params=pltpu.CompilerParams(vmem_limit_bytes=VMEM_LIMIT),
        cost_estimate=pl.CostEstimate(
            flops=2 * seq * width * total,
            bytes_accessed=2 * (2 * total * width + seq * total),
            transcendentals=0,
        ),
        name="branch_part",
    )(pos, attended, *[cat] * 4, *[oth] * 4)


def grads_kernel(
    pos, g0, gp, ga, gb, gm, att_ref, w_ref, keep, send, out_ref, att_s, rows_s, acc
):
    piece = keep.shape[3]
    c, m = pos[0], pos[1]
    rows = g0.shape[0]
    half = rows // 2
    step = pl.program_id(0)

    @pl.when(step == 0)
    def _():
        turn_tokens(pos, att_ref, att_s)
        acc[...] = jnp.zeros_like(acc)

    rows_s[pl.ds(0, rows), :] = g0[...]
    rows_s[pl.ds(rows, rows), :] = gp[...]
    rows_s[pl.ds(2 * rows, half), :] = ga[...]
    rows_s[pl.ds(2 * rows + half, half), :] = gb[...]
    rows_s[pl.ds(3 * rows, rows), :] = gm[...]
    acc[...] += jnp.dot(rows_s[...], w_ref[...], preferred_element_type=F32)
    prod = lax.dot_general(
        rows_s[...], att_s[...], (((0,), (0,)), ((), ())), preferred_element_type=F32
    ).astype(BF)
    for w in range(2):
        for y in range(4):
            i = w * 4 + y
            even = prod[2 * i * piece : (2 * i + 1) * piece]
            odd = prod[(2 * i + 1) * piece : (2 * i + 2) * piece]
            far, near = place(c, step, y)
            keep[far, near, w] = jnp.where(c == 0, even, odd)
            send[near, far, w] = jnp.where(c == 0, odd, even)

    @pl.when(step == pl.num_programs(0) - 1)
    def _():
        for k in range(4):
            start = pl.multiple_of(((m + k) % 4) * rows, 16)
            out_ref[pl.ds(start, rows), :] = acc[pl.ds(k * rows, rows), :].astype(BF)


def grads_part(pos, g0, gp, ga, gb, gm, attended, weight, piece):
    total, width = weight.shape
    seq = attended.shape[0]
    span = 16 * piece
    shape = (4, 4, 2, piece, width)
    sds = jax.ShapeDtypeStruct
    whole = pl.BlockSpec((seq, width), lambda i: (0, 0))
    block = pl.BlockSpec(shape, lambda i: (0, 0, 0, 0, 0))
    return pl.pallas_call(
        grads_kernel,
        grid=(4,),
        in_specs=[pl.BlockSpec(memory_space=pltpu.SMEM)]
        + [pl.BlockSpec((g.shape[0], span), lambda i: (0, i)) for g in (g0, gp, ga, gb, gm)]
        + [whole, pl.BlockSpec((span, width), lambda i: (i, 0))],
        out_specs=[block, block, whole],
        out_shape=[
            sds(shape, BF),
            sds(shape, BF),
            sds((seq, width), BF),
        ],
        scratch_shapes=[
            pltpu.VMEM((seq, width), BF),
            pltpu.VMEM((seq, span), BF),
            pltpu.VMEM((seq, width), F32),
        ],
        compiler_params=pltpu.CompilerParams(vmem_limit_bytes=VMEM_LIMIT),
        cost_estimate=pl.CostEstimate(
            flops=4 * seq * width * total,
            bytes_accessed=2 * (2 * total * width + seq * total),
            transcendentals=0,
        ),
        name="grads_part",
    )(pos, g0, gp, ga, gb, gm, attended, weight)


def sum_f32(*parts):
    total = parts[0].astype(F32)
    for part in parts[1:]:
        total = total + part.astype(F32)
    return total


def on_device(query, key, value, residual, cotangent, out_weight, norm_gain, doc_ids):
    seq, width = query.shape
    heads = width // HD
    piece = out_weight.shape[0]
    rows, d_model = residual.shape
    half = rows // 2
    scale = 1.0 / math.sqrt(HD)
    dp = lax.axis_index("dp")
    w, c = dp // 8 % 2, dp % 2
    m = lax.axis_index("mp")
    pos = jnp.stack([c, m]).astype(jnp.int32)

    across = swap(out_weight, FLIP_W)
    pair = jnp.where(w == 0, jnp.stack([out_weight, across]), jnp.stack([across, out_weight]))
    cat = exchange(spread(exchange(spread(pair), NEAR)), FAR)

    query3 = query.reshape(seq, heads, HD)
    key3 = key.reshape(seq, heads, HD)
    value3 = value.reshape(seq, heads, HD)
    probs = attention_probs(query3, key3, doc_ids)
    probs_b = probs.astype(BF)
    attended = jnp.einsum("hts,shd->thd", probs_b, value3, preferred_element_type=F32)
    attended = attended.astype(BF).reshape(seq, width)

    cat, attended = lax.optimization_barrier((cat, attended))
    oth = swap(cat, FLIP_C)
    weight, p0, p1a, p1b, p2a, p2b, p3a, p3b = branch_part(pos, attended, cat, oth)
    ra = send_mp(p2a, 1)
    rb = send_mp(p2b, -1)
    up_b = send_mp(p1b, 1)
    down_a = send_mp(p3a, -1)
    up_a = send_mp(sum_f32(p1a, ra).astype(BF), 1)
    down_b = send_mp(sum_f32(p3b, rb).astype(BF), -1)
    up = jnp.concatenate([up_a, up_b])
    down = jnp.concatenate([down_a, down_b])
    mixed = sum_f32(residual, p0, up, down)
    cot = cotangent.astype(F32)
    gscaled = cot * norm_gain
    inv = lax.rsqrt(jnp.mean(mixed * mixed, axis=1, keepdims=True) + 1e-05)
    mean_dot = jnp.mean(gscaled * mixed, axis=1, keepdims=True)
    grad_residual = (inv * (gscaled - mixed * inv * inv * mean_dot)).astype(BF)

    tie = lax.optimization_barrier

    def add_from(total, bits):
        for bit in bits:
            total = total + swap(total, [(i, i ^ bit) for i in range(64)])
        return total

    gain = jnp.sum(cot * mixed * inv, axis=0).reshape(d_model // 128, 128)
    gm = send_mp(grad_residual, 1)
    gp = send_mp(grad_residual, -1)
    gm, gp, gain = tie((gm, gp, add_from(gain, (1, 2, 4))))
    ga = send_mp(gm[:half], 1)
    gb = send_mp(gp[half:], -1)
    ga, gb, gain = tie((ga, gb, add_from(gain, (16, 32))))
    keep, send, grad_attended = grads_part(
        pos, grad_residual, gp, ga, gb, gm, attended, weight, piece
    )
    both = sum_f32(keep, swap(send, FLIP_C)).astype(BF)
    part = exchange(both, FAR)
    gain = add_from(gain, (8,))
    for bit in (1, 2):
        gain = gain + lax.ppermute(gain, "mp", [(i, i ^ bit) for i in range(4)])
    part, gain = tie((part, gain))
    part = jnp.sum(part.astype(F32), axis=0).astype(BF)
    total = jnp.sum(exchange(part, NEAR).astype(F32), axis=0) / 64
    home = jnp.where(w == 0, total[0], total[1])
    away = jnp.where(w == 0, total[1], total[0]).astype(BF)
    grad_weight = home + swap(away, FLIP_W).astype(F32)
    grad_gain = lax.dynamic_slice_in_dim(gain.reshape(d_model) / 64, dp * piece, piece, 0)

    grad3 = grad_attended.reshape(seq, heads, HD)
    grad_value = jnp.einsum("hts,thd->shd", probs_b, grad3, preferred_element_type=F32)
    grad_value = grad_value.astype(BF).reshape(seq, width)
    grad_probs = jnp.einsum("thd,shd->hts", grad3, value3, preferred_element_type=F32)
    delta = jnp.sum(probs * grad_probs, axis=2, keepdims=True)
    grad_scores = (probs * (grad_probs - delta)).astype(BF)
    grad_query = jnp.einsum("hts,shd->thd", grad_scores, key3, preferred_element_type=F32) * scale
    grad_key = jnp.einsum("hts,thd->shd", grad_scores, query3, preferred_element_type=F32) * scale
    grad_query = grad_query.astype(BF).reshape(seq, width)
    grad_key = grad_key.astype(BF).reshape(seq, width)
    return (grad_query, grad_key, grad_value, grad_residual, grad_weight, grad_gain)


def solution(mesh):
    placed = (
        P("dp", "mp"),
        P("dp", "mp"),
        P("dp", "mp"),
        P(("dp", "mp"), None),
        P(("dp", "mp"), None),
        P("dp", "mp"),
        P(),
        P("dp"),
    )
    return jax.shard_map(
        on_device,
        mesh=mesh,
        in_specs=placed,
        out_specs=(
            P("dp", "mp"),
            P("dp", "mp"),
            P("dp", "mp"),
            P(("dp", "mp"), None),
            P("dp", "mp"),
            P("dp"),
        ),
        check_vma=False,
    )
```

```python
import math

import jax
import jax.numpy as jnp
from jax import lax
from jax.experimental import pallas as pl
from jax.experimental.pallas import tpu as pltpu
from jax.sharding import PartitionSpec as P

HD = 128
BF = jnp.bfloat16
F32 = jnp.float32
VMEM_LIMIT = 40 * 1024 * 1024


def rings(along_y):
    groups = []
    for c in range(2):
        for w in range(2):
            for line in range(4):
                places = [(line, k) if (c == 0) == along_y else (k, line) for k in range(4)]
                groups.append([((x * 2 + w) * 4 + y) * 2 + c for x, y in places])
    return groups


FAR = rings(False)
NEAR = [
    [i ^ flip for i in group for flip in (0, 8)] for group in rings(True) if not group[0] & 8
]
FLIP_C = [(i, i ^ 1) for i in range(64)]


def swap(value, pairs):
    return lax.ppermute(value, "dp", pairs)


def send_mp(value, step):
    return lax.ppermute(value, "mp", [(i, (i + step) % 4) for i in range(4)])


def exchange(blocks, groups):
    return lax.all_to_all(blocks, "dp", 0, 0, axis_index_groups=groups)


def spread(block, copies):
    return jnp.broadcast_to(block[None], (copies, *block.shape))


def attention_probs(query3, key3, doc_ids):
    seq = query3.shape[0]
    scale = 1.0 / math.sqrt(HD)
    scores = jnp.einsum("thd,shd->hts", query3, key3, preferred_element_type=F32) * scale
    pos = lax.iota(jnp.int32, seq)
    allowed = (pos[None, :] <= pos[:, None]) & (doc_ids[None, :] == doc_ids[:, None])
    scores = jnp.where(allowed[None], scores, -1e30)
    top = jnp.max(scores, axis=2, keepdims=True)
    weights = jnp.exp(scores - top)
    return weights / jnp.sum(weights, axis=2, keepdims=True)


def turn_tokens(pos, att_ref, att_s):
    rows = att_ref.shape[0] // 4
    for k in range(4):
        start = pl.multiple_of(((pos[1] + k) % 4) * rows, 16)
        att_s[pl.ds(k * rows, rows), :] = att_ref[pl.ds(start, rows), :]


def place(c, x, y):
    return jnp.where(c == 0, x, y), jnp.where(c == 0, y, x)


def assemble(c, mine, other, w_s):
    piece = mine[0].shape[3]
    for w in range(2):
        for y in range(4):
            i = 2 * (w * 4 + y)
            w_s[pl.ds(pl.multiple_of((i + c) * piece, 16), piece), :] = mine[y][0, 0, w]
            w_s[pl.ds(pl.multiple_of((i + 1 - c) * piece, 16), piece), :] = other[y][0, 0, w]


def weight_specs(piece, width):
    def block(flip, y):
        def at(i, pos):
            return *place(pos[0] ^ flip, i, y), 0, 0, 0

        return pl.BlockSpec((1, 1, 2, piece, width), at)

    return [block(flip, y) for flip in range(2) for y in range(4)]


def branch_kernel(pos, att_ref, *refs):
    p0, p1a, p3b, up, down, att_s, w_s = refs[8:]
    rows = att_ref.shape[0] // 4
    half = rows // 2

    @pl.when(pl.program_id(0) == 0)
    def _():
        turn_tokens(pos, att_ref, att_s)

    assemble(pos[0], refs[:4], refs[4:8], w_s)
    prod = lax.dot_general(
        att_s[...], w_s[...], (((1,), (1,)), ((), ())), preferred_element_type=F32
    ).astype(BF)
    p0[...] = prod[:rows]
    p1a[...] = prod[rows : rows + half]
    p3b[...] = prod[3 * rows + half :]
    up[pl.ds(0, half), :] = prod[2 * rows : 2 * rows + half]
    up[pl.ds(half, half), :] = prod[rows + half : 2 * rows]
    down[pl.ds(0, half), :] = prod[2 * rows + half : 3 * rows]
    down[pl.ds(half, half), :] = prod[3 * rows : 3 * rows + half]


def branch_part(pos, attended, cat, oth):
    piece, width = cat.shape[3:]
    seq = attended.shape[0]
    rows, span = seq // 4, 16 * piece
    total = 4 * span
    heights = (rows, rows // 2, rows // 2, rows, rows)
    return pl.pallas_call(
        branch_kernel,
        grid_spec=pltpu.PrefetchScalarGridSpec(
            num_scalar_prefetch=1,
            grid=(4,),
            in_specs=[pl.BlockSpec((seq, width), lambda i, pos: (0, 0))]
            + weight_specs(piece, width),
            out_specs=[pl.BlockSpec((h, span), lambda i, pos: (0, i)) for h in heights],
            scratch_shapes=[pltpu.VMEM((seq, width), BF), pltpu.VMEM((span, width), BF)],
        ),
        out_shape=[jax.ShapeDtypeStruct((h, total), BF) for h in heights],
        compiler_params=pltpu.CompilerParams(vmem_limit_bytes=VMEM_LIMIT),
        cost_estimate=pl.CostEstimate(
            flops=2 * seq * width * total,
            bytes_accessed=2 * (total * width + seq * total),
            transcendentals=0,
        ),
        name="branch_part",
    )(pos, attended, *[cat] * 4, *[oth] * 4)


def gather_rows(g0, gp, ga, gb, gm, rows_s):
    rows = g0.shape[0]
    half = rows // 2
    rows_s[pl.ds(0, rows), :] = g0[...]
    rows_s[pl.ds(rows, rows), :] = gp[...]
    rows_s[pl.ds(2 * rows, half), :] = ga[...]
    rows_s[pl.ds(2 * rows + half, half), :] = gb[...]
    rows_s[pl.ds(3 * rows, rows), :] = gm[...]


def weight_kernel(pos, g0, gp, ga, gb, gm, att_ref, keep, send, att_s, rows_s):
    piece = keep.shape[3]
    c = pos[0]
    step = pl.program_id(0)

    @pl.when(step == 0)
    def _():
        turn_tokens(pos, att_ref, att_s)

    gather_rows(g0, gp, ga, gb, gm, rows_s)
    prod = lax.dot_general(
        rows_s[...], att_s[...], (((0,), (0,)), ((), ())), preferred_element_type=F32
    ).astype(BF)
    for w in range(2):
        for y in range(4):
            i = 2 * (w * 4 + y)
            even = prod[i * piece : (i + 1) * piece]
            odd = prod[(i + 1) * piece : (i + 2) * piece]
            far, near = place(c, step, y)
            keep[far, near, w] = jnp.where(c == 0, even, odd)
            send[near, far, w] = jnp.where(c == 0, odd, even)


def weight_part(pos, parts, attended, piece):
    seq, width = attended.shape
    span = 16 * piece
    shape = (4, 4, 2, piece, width)
    block = pl.BlockSpec(shape, lambda i: (0, 0, 0, 0, 0))
    return pl.pallas_call(
        weight_kernel,
        grid=(4,),
        in_specs=[pl.BlockSpec(memory_space=pltpu.SMEM)]
        + [pl.BlockSpec((g.shape[0], span), lambda i: (0, i)) for g in parts]
        + [pl.BlockSpec((seq, width), lambda i: (0, 0))],
        out_specs=[block, block],
        out_shape=[jax.ShapeDtypeStruct(shape, BF)] * 2,
        scratch_shapes=[pltpu.VMEM((seq, width), BF), pltpu.VMEM((seq, span), BF)],
        compiler_params=pltpu.CompilerParams(vmem_limit_bytes=VMEM_LIMIT),
        cost_estimate=pl.CostEstimate(
            flops=8 * seq * width * span,
            bytes_accessed=8 * (span * width + seq * span),
            transcendentals=0,
        ),
        name="weight_part",
    )(pos, *parts, attended)


def attended_kernel(pos, g0, gp, ga, gb, gm, *refs):
    out_ref, rows_s, w_s, acc = refs[8:]
    m = pos[1]
    rows = g0.shape[0]
    step = pl.program_id(0)

    @pl.when(step == 0)
    def _():
        acc[...] = jnp.zeros_like(acc)

    gather_rows(g0, gp, ga, gb, gm, rows_s)
    assemble(pos[0], refs[:4], refs[4:8], w_s)
    acc[...] += jnp.dot(rows_s[...], w_s[...], preferred_element_type=F32)

    @pl.when(step == pl.num_programs(0) - 1)
    def _():
        for k in range(4):
            start = pl.multiple_of(((m + k) % 4) * rows, 16)
            out_ref[pl.ds(start, rows), :] = acc[pl.ds(k * rows, rows), :].astype(BF)


def attended_part(pos, parts, cat, oth):
    piece, width = cat.shape[3:]
    seq = 4 * parts[0].shape[0]
    span = 16 * piece
    return pl.pallas_call(
        attended_kernel,
        grid_spec=pltpu.PrefetchScalarGridSpec(
            num_scalar_prefetch=1,
            grid=(4,),
            in_specs=[pl.BlockSpec((g.shape[0], span), lambda i, pos: (0, i)) for g in parts]
            + weight_specs(piece, width),
            out_specs=pl.BlockSpec((seq, width), lambda i, pos: (0, 0)),
            scratch_shapes=[
                pltpu.VMEM((seq, span), BF),
                pltpu.VMEM((span, width), BF),
                pltpu.VMEM((seq, width), F32),
            ],
        ),
        out_shape=jax.ShapeDtypeStruct((seq, width), BF),
        compiler_params=pltpu.CompilerParams(vmem_limit_bytes=VMEM_LIMIT),
        cost_estimate=pl.CostEstimate(
            flops=8 * seq * width * span,
            bytes_accessed=8 * (span * width + seq * span),
            transcendentals=0,
        ),
        name="attended_part",
    )(pos, *parts, *[cat] * 4, *[oth] * 4)


def sum_f32(*parts):
    total = parts[0].astype(F32)
    for part in parts[1:]:
        total = total + part.astype(F32)
    return total


def on_device(query, key, value, residual, cotangent, out_weight, norm_gain, doc_ids):
    seq, width = query.shape
    heads = width // HD
    piece = out_weight.shape[0]
    rows, d_model = residual.shape
    half = rows // 2
    scale = 1.0 / math.sqrt(HD)
    dp = lax.axis_index("dp")
    c = dp % 2
    m = lax.axis_index("mp")
    pos = jnp.stack([c, m]).astype(jnp.int32)

    planes = exchange(spread(out_weight, 8), NEAR).reshape(4, 2, piece, width)
    cat = exchange(spread(planes, 4), FAR)

    query3 = query.reshape(seq, heads, HD)
    key3 = key.reshape(seq, heads, HD)
    value3 = value.reshape(seq, heads, HD)
    probs = attention_probs(query3, key3, doc_ids)
    probs_b = probs.astype(BF)
    attended = jnp.einsum("hts,shd->thd", probs_b, value3, preferred_element_type=F32)
    attended = attended.astype(BF).reshape(seq, width)

    cat, attended = lax.optimization_barrier((cat, attended))
    oth = swap(cat, FLIP_C)
    p0, p1a, p3b, up, down = branch_part(pos, attended, cat, oth)
    up, down = send_mp(up, 1), send_mp(down, -1)
    up_a = send_mp(sum_f32(p1a, up[:half]).astype(BF), 1)
    down_b = send_mp(sum_f32(p3b, down[:half]).astype(BF), -1)
    up = jnp.concatenate([up_a, up[half:]])
    down = jnp.concatenate([down[half:], down_b])
    mixed = sum_f32(residual, p0, up, down)
    cot = cotangent.astype(F32)
    gscaled = cot * norm_gain
    inv = lax.rsqrt(jnp.mean(mixed * mixed, axis=1, keepdims=True) + 1e-05)
    mean_dot = jnp.mean(gscaled * mixed, axis=1, keepdims=True)
    grad_residual = (inv * (gscaled - mixed * inv * inv * mean_dot)).astype(BF)

    tie = lax.optimization_barrier

    def add_from(total, bits):
        for bit in bits:
            total = total + swap(total, [(i, i ^ bit) for i in range(64)])
        return total

    gain = jnp.sum(cot * mixed * inv, axis=0).reshape(d_model // 128, 128)
    gm = send_mp(grad_residual, 1)
    gp = send_mp(grad_residual, -1)
    gm, gp, gain = tie((gm, gp, add_from(gain, (1, 2, 4))))
    ga = send_mp(gm[:half], 1)
    gb = send_mp(gp[half:], -1)
    ga, gb, gain = tie((ga, gb, add_from(gain, (16, 32))))
    parts = (grad_residual, gp, ga, gb, gm)
    keep, send = weight_part(pos, parts, attended, piece)
    both = sum_f32(keep, swap(send, FLIP_C)).astype(BF)
    grad_attended = attended_part(pos, parts, cat, oth)
    part = exchange(both, FAR)
    gain = add_from(gain, (8,))
    for bit in (1, 2):
        gain = gain + lax.ppermute(gain, "mp", [(i, i ^ bit) for i in range(4)])
    part, gain = tie((part, gain))
    part = sum_f32(*part).astype(BF).reshape(8, piece, width)
    grad_weight = sum_f32(*exchange(part, NEAR)) / 64
    grad_gain = lax.dynamic_slice_in_dim(gain.reshape(d_model) / 64, dp * piece, piece, 0)

    grad3 = grad_attended.reshape(seq, heads, HD)
    grad_value = jnp.einsum("hts,thd->shd", probs_b, grad3, preferred_element_type=F32)
    grad_value = grad_value.astype(BF).reshape(seq, width)
    grad_probs = jnp.einsum("thd,shd->hts", grad3, value3, preferred_element_type=F32)
    delta = jnp.sum(probs * grad_probs, axis=2, keepdims=True)
    grad_scores = (probs * (grad_probs - delta)).astype(BF)
    grad_query = jnp.einsum("hts,shd->thd", grad_scores, key3, preferred_element_type=F32) * scale
    grad_key = jnp.einsum("hts,thd->shd", grad_scores, query3, preferred_element_type=F32) * scale
    grad_query = grad_query.astype(BF).reshape(seq, width)
    grad_key = grad_key.astype(BF).reshape(seq, width)
    return (grad_query, grad_key, grad_value, grad_residual, grad_weight, grad_gain)


def solution(mesh):
    placed = (
        P("dp", "mp"),
        P("dp", "mp"),
        P("dp", "mp"),
        P(("dp", "mp"), None),
        P(("dp", "mp"), None),
        P("dp", "mp"),
        P(),
        P("dp"),
    )
    return jax.shard_map(
        on_device,
        mesh=mesh,
        in_specs=placed,
        out_specs=(
            P("dp", "mp"),
            P("dp", "mp"),
            P("dp", "mp"),
            P(("dp", "mp"), None),
            P("dp", "mp"),
            P("dp"),
        ),
        check_vma=False,
    )
```

```python
import math

import jax
import jax.numpy as jnp
from jax import lax
from jax.experimental import pallas as pl
from jax.experimental.pallas import tpu as pltpu
from jax.sharding import PartitionSpec as P

HD = 128
BF = jnp.bfloat16
F32 = jnp.float32
VMEM_LIMIT = 40 * 1024 * 1024


def rings(along_y):
    groups = []
    for c in range(2):
        for w in range(2):
            for line in range(4):
                places = [(line, k) if (c == 0) == along_y else (k, line) for k in range(4)]
                groups.append([((x * 2 + w) * 4 + y) * 2 + c for x, y in places])
    return groups


FAR = rings(False)
NEAR = [
    [i ^ flip for i in group for flip in (0, 8)] for group in rings(True) if not group[0] & 8
]
FLIP_C = [(i, i ^ 1) for i in range(64)]


def swap(value, pairs):
    return lax.ppermute(value, "dp", pairs)


def send_mp(value, step):
    return lax.ppermute(value, "mp", [(i, (i + step) % 4) for i in range(4)])


def exchange(blocks, groups):
    return lax.all_to_all(blocks, "dp", 0, 0, axis_index_groups=groups)


def spread(block, copies):
    return jnp.broadcast_to(block[None], (copies, *block.shape))


def attention_probs(query3, key3, doc_ids):
    seq = query3.shape[0]
    scale = 1.0 / math.sqrt(HD)
    scores = jnp.einsum("thd,shd->hts", query3, key3, preferred_element_type=F32) * scale
    pos = lax.iota(jnp.int32, seq)
    allowed = (pos[None, :] <= pos[:, None]) & (doc_ids[None, :] == doc_ids[:, None])
    scores = jnp.where(allowed[None], scores, -1e30)
    top = jnp.max(scores, axis=2, keepdims=True)
    weights = jnp.exp(scores - top)
    return weights / jnp.sum(weights, axis=2, keepdims=True)


def turn_tokens(pos, att_ref, att_s):
    rows = att_ref.shape[0] // 4
    for k in range(4):
        start = pl.multiple_of(((pos[1] + k) % 4) * rows, 16)
        att_s[pl.ds(k * rows, rows), :] = att_ref[pl.ds(start, rows), :]


def place(c, x, y):
    return jnp.where(c == 0, x, y), jnp.where(c == 0, y, x)


def assemble(c, mine, other, w_s):
    piece = mine[0].shape[3]
    for w in range(2):
        for y in range(4):
            i = 2 * (w * 4 + y)
            w_s[pl.ds(pl.multiple_of((i + c) * piece, 16), piece), :] = mine[y][0, 0, w]
            w_s[pl.ds(pl.multiple_of((i + 1 - c) * piece, 16), piece), :] = other[y][0, 0, w]


def weight_specs(piece, width):
    def block(flip, y):
        def at(i, pos):
            return *place(pos[0] ^ flip, i, y), 0, 0, 0

        return pl.BlockSpec((1, 1, 2, piece, width), at)

    return [block(flip, y) for flip in range(2) for y in range(4)]


def branch_kernel(pos, att_ref, *refs):
    p0, p1a, p3b, up, down, att_s, w_s = refs[8:]
    rows = att_ref.shape[0] // 4
    half = rows // 2

    @pl.when(pl.program_id(0) == 0)
    def _():
        turn_tokens(pos, att_ref, att_s)

    assemble(pos[0], refs[:4], refs[4:8], w_s)
    prod = lax.dot_general(
        att_s[...], w_s[...], (((1,), (1,)), ((), ())), preferred_element_type=F32
    ).astype(BF)
    p0[...] = prod[:rows]
    p1a[...] = prod[rows : rows + half]
    p3b[...] = prod[3 * rows + half :]
    up[pl.ds(0, half), :] = prod[2 * rows : 2 * rows + half]
    up[pl.ds(half, half), :] = prod[rows + half : 2 * rows]
    down[pl.ds(0, half), :] = prod[2 * rows + half : 3 * rows]
    down[pl.ds(half, half), :] = prod[3 * rows : 3 * rows + half]


def branch_part(pos, attended, cat, oth):
    piece, width = cat.shape[3:]
    seq = attended.shape[0]
    rows, span = seq // 4, 16 * piece
    total = 4 * span
    heights = (rows, rows // 2, rows // 2, rows, rows)
    return pl.pallas_call(
        branch_kernel,
        grid_spec=pltpu.PrefetchScalarGridSpec(
            num_scalar_prefetch=1,
            grid=(4,),
            in_specs=[pl.BlockSpec((seq, width), lambda i, pos: (0, 0))]
            + weight_specs(piece, width),
            out_specs=[pl.BlockSpec((h, span), lambda i, pos: (0, i)) for h in heights],
            scratch_shapes=[pltpu.VMEM((seq, width), BF), pltpu.VMEM((span, width), BF)],
        ),
        out_shape=[jax.ShapeDtypeStruct((h, total), BF) for h in heights],
        compiler_params=pltpu.CompilerParams(vmem_limit_bytes=VMEM_LIMIT),
        cost_estimate=pl.CostEstimate(
            flops=2 * seq * width * total,
            bytes_accessed=2 * (total * width + seq * total),
            transcendentals=0,
        ),
        name="branch_part",
    )(pos, attended, *[cat] * 4, *[oth] * 4)


def gather_rows(g0, gp, ga, gb, gm, rows_s):
    rows = g0.shape[0]
    half = rows // 2
    rows_s[pl.ds(0, rows), :] = g0[...]
    rows_s[pl.ds(rows, rows), :] = gp[...]
    rows_s[pl.ds(2 * rows, half), :] = ga[...]
    rows_s[pl.ds(2 * rows + half, half), :] = gb[...]
    rows_s[pl.ds(3 * rows, rows), :] = gm[...]


def weight_kernel(pos, g0, gp, ga, gb, gm, att_ref, keep, send, att_s, rows_s):
    piece = keep.shape[3]
    c = pos[0]
    step = pl.program_id(0)

    @pl.when(step == 0)
    def _():
        turn_tokens(pos, att_ref, att_s)

    gather_rows(g0, gp, ga, gb, gm, rows_s)
    prod = lax.dot_general(
        rows_s[...], att_s[...], (((0,), (0,)), ((), ())), preferred_element_type=F32
    ).astype(BF)
    for w in range(2):
        for y in range(4):
            i = 2 * (w * 4 + y)
            even = prod[i * piece : (i + 1) * piece]
            odd = prod[(i + 1) * piece : (i + 2) * piece]
            far, near = place(c, step, y)
            keep[far, near, w] = jnp.where(c == 0, even, odd)
            send[near, far, w] = jnp.where(c == 0, odd, even)


def weight_part(pos, parts, attended, piece):
    seq, width = attended.shape
    span = 16 * piece
    shape = (4, 4, 2, piece, width)
    block = pl.BlockSpec(memory_space=pltpu.VMEM)
    return pl.pallas_call(
        weight_kernel,
        grid=(4,),
        in_specs=[pl.BlockSpec(memory_space=pltpu.SMEM)]
        + [pl.BlockSpec((g.shape[0], span), lambda i: (0, i)) for g in parts]
        + [pl.BlockSpec((seq, width), lambda i: (0, 0))],
        out_specs=[block, block],
        out_shape=[jax.ShapeDtypeStruct(shape, BF)] * 2,
        scratch_shapes=[pltpu.VMEM((seq, width), BF), pltpu.VMEM((seq, span), BF)],
        compiler_params=pltpu.CompilerParams(vmem_limit_bytes=VMEM_LIMIT),
        cost_estimate=pl.CostEstimate(
            flops=8 * seq * width * span,
            bytes_accessed=8 * (span * width + seq * span),
            transcendentals=0,
        ),
        name="weight_part",
    )(pos, *parts, attended)


def attended_kernel(pos, g0, gp, ga, gb, gm, *refs):
    out_ref, rows_s, w_s, acc = refs[8:]
    m = pos[1]
    rows = g0.shape[0]
    step = pl.program_id(0)

    @pl.when(step == 0)
    def _():
        acc[...] = jnp.zeros_like(acc)

    gather_rows(g0, gp, ga, gb, gm, rows_s)
    assemble(pos[0], refs[:4], refs[4:8], w_s)
    acc[...] += jnp.dot(rows_s[...], w_s[...], preferred_element_type=F32)

    @pl.when(step == pl.num_programs(0) - 1)
    def _():
        for k in range(4):
            start = pl.multiple_of(((m + k) % 4) * rows, 16)
            out_ref[pl.ds(start, rows), :] = acc[pl.ds(k * rows, rows), :].astype(BF)


def attended_part(pos, parts, cat, oth):
    piece, width = cat.shape[3:]
    seq = 4 * parts[0].shape[0]
    span = 16 * piece
    return pl.pallas_call(
        attended_kernel,
        grid_spec=pltpu.PrefetchScalarGridSpec(
            num_scalar_prefetch=1,
            grid=(4,),
            in_specs=[pl.BlockSpec((g.shape[0], span), lambda i, pos: (0, i)) for g in parts]
            + weight_specs(piece, width),
            out_specs=pl.BlockSpec((seq, width), lambda i, pos: (0, 0)),
            scratch_shapes=[
                pltpu.VMEM((seq, span), BF),
                pltpu.VMEM((span, width), BF),
                pltpu.VMEM((seq, width), F32),
            ],
        ),
        out_shape=jax.ShapeDtypeStruct((seq, width), BF),
        compiler_params=pltpu.CompilerParams(vmem_limit_bytes=VMEM_LIMIT),
        cost_estimate=pl.CostEstimate(
            flops=8 * seq * width * span,
            bytes_accessed=8 * (span * width + seq * span),
            transcendentals=0,
        ),
        name="attended_part",
    )(pos, *parts, *[cat] * 4, *[oth] * 4)


def sum_kernel(in_ref, out_ref):
    total = in_ref[0].astype(F32)
    for k in range(1, 4):
        total = total + in_ref[k].astype(F32)
    out_ref[...] = total.astype(BF)


def sum_blocks(blocks):
    piece, width = blocks.shape[3:]
    return pl.pallas_call(
        sum_kernel,
        grid=(4,),
        in_specs=[pl.BlockSpec((4, 1, 2, piece, width), lambda i: (0, i, 0, 0, 0))],
        out_specs=pl.BlockSpec((1, 2, piece, width), lambda i: (i, 0, 0, 0)),
        out_shape=jax.ShapeDtypeStruct((4, 2, piece, width), BF),
        compiler_params=pltpu.CompilerParams(vmem_limit_bytes=VMEM_LIMIT),
        cost_estimate=pl.CostEstimate(
            flops=32 * piece * width, bytes_accessed=80 * piece * width, transcendentals=0
        ),
        name="sum_blocks",
    )(blocks)


def sum_f32(*parts):
    total = parts[0].astype(F32)
    for part in parts[1:]:
        total = total + part.astype(F32)
    return total


def on_device(query, key, value, residual, cotangent, out_weight, norm_gain, doc_ids):
    seq, width = query.shape
    heads = width // HD
    piece = out_weight.shape[0]
    rows, d_model = residual.shape
    half = rows // 2
    scale = 1.0 / math.sqrt(HD)
    dp = lax.axis_index("dp")
    c = dp % 2
    m = lax.axis_index("mp")
    pos = jnp.stack([c, m]).astype(jnp.int32)

    planes = exchange(spread(out_weight, 8), NEAR).reshape(4, 2, piece, width)
    cat = exchange(spread(planes, 4), FAR)

    query3 = query.reshape(seq, heads, HD)
    key3 = key.reshape(seq, heads, HD)
    value3 = value.reshape(seq, heads, HD)
    probs = attention_probs(query3, key3, doc_ids)
    probs_b = probs.astype(BF)
    attended = jnp.einsum("hts,shd->thd", probs_b, value3, preferred_element_type=F32)
    attended = attended.astype(BF).reshape(seq, width)

    cat, attended = lax.optimization_barrier((cat, attended))
    oth = swap(cat, FLIP_C)
    p0, p1a, p3b, up, down = branch_part(pos, attended, cat, oth)
    up, down = send_mp(up, 1), send_mp(down, -1)
    up_a = send_mp(sum_f32(p1a, up[:half]).astype(BF), 1)
    down_b = send_mp(sum_f32(p3b, down[:half]).astype(BF), -1)
    up = jnp.concatenate([up_a, up[half:]])
    down = jnp.concatenate([down[half:], down_b])
    mixed = sum_f32(residual, p0, up, down)
    cot = cotangent.astype(F32)
    gscaled = cot * norm_gain
    inv = lax.rsqrt(jnp.mean(mixed * mixed, axis=1, keepdims=True) + 1e-05)
    mean_dot = jnp.mean(gscaled * mixed, axis=1, keepdims=True)
    grad_residual = (inv * (gscaled - mixed * inv * inv * mean_dot)).astype(BF)

    tie = lax.optimization_barrier

    def add_from(total, bits):
        for bit in bits:
            total = total + swap(total, [(i, i ^ bit) for i in range(64)])
        return total

    gain = jnp.sum(cot * mixed * inv, axis=0).reshape(d_model // 128, 128)
    gm = send_mp(grad_residual, 1)
    gp = send_mp(grad_residual, -1)
    gm, gp, gain = tie((gm, gp, add_from(gain, (2, 4, 16, 32))))
    ga = send_mp(gm[:half], 1)
    gb = send_mp(gp[half:], -1)
    parts = (grad_residual, gp, ga, gb, gm)
    keep, send = weight_part(pos, parts, attended, piece)
    swapped, grad_attended = tie((swap(send, FLIP_C), attended_part(pos, parts, cat, oth)))
    both = sum_f32(keep, swapped).astype(BF)
    part = exchange(both, FAR)
    gain = add_from(gain, (1, 8))
    for bit in (1, 2):
        gain = gain + lax.ppermute(gain, "mp", [(i, i ^ bit) for i in range(4)])
    part, gain = tie((part, gain))
    part = sum_blocks(part).reshape(8, piece, width)
    grad_weight = sum_f32(*exchange(part, NEAR)) / 64
    grad_gain = lax.dynamic_slice_in_dim(gain.reshape(d_model) / 64, dp * piece, piece, 0)

    grad3 = grad_attended.reshape(seq, heads, HD)
    grad_value = jnp.einsum("hts,thd->shd", probs_b, grad3, preferred_element_type=F32)
    grad_value = grad_value.astype(BF).reshape(seq, width)
    grad_probs = jnp.einsum("thd,shd->hts", grad3, value3, preferred_element_type=F32)
    delta = jnp.sum(probs * grad_probs, axis=2, keepdims=True)
    grad_scores = (probs * (grad_probs - delta)).astype(BF)
    grad_query = jnp.einsum("hts,shd->thd", grad_scores, key3, preferred_element_type=F32) * scale
    grad_key = jnp.einsum("hts,thd->shd", grad_scores, query3, preferred_element_type=F32) * scale
    grad_query = grad_query.astype(BF).reshape(seq, width)
    grad_key = grad_key.astype(BF).reshape(seq, width)
    return (grad_query, grad_key, grad_value, grad_residual, grad_weight, grad_gain)


def solution(mesh):
    placed = (
        P("dp", "mp"),
        P("dp", "mp"),
        P("dp", "mp"),
        P(("dp", "mp"), None),
        P(("dp", "mp"), None),
        P("dp", "mp"),
        P(),
        P("dp"),
    )
    return jax.shard_map(
        on_device,
        mesh=mesh,
        in_specs=placed,
        out_specs=(
            P("dp", "mp"),
            P("dp", "mp"),
            P("dp", "mp"),
            P(("dp", "mp"), None),
            P("dp", "mp"),
            P("dp"),
        ),
        check_vma=False,
    )
```

```python
import math

import jax
import jax.numpy as jnp
from jax import lax
from jax.experimental import pallas as pl
from jax.experimental.pallas import tpu as pltpu
from jax.sharding import PartitionSpec as P

HD = 128
BF = jnp.bfloat16
F32 = jnp.float32
VMEM_LIMIT = 40 * 1024 * 1024


def rings(along_y):
    groups = []
    for c in range(2):
        for w in range(2):
            for line in range(4):
                places = [(line, k) if (c == 0) == along_y else (k, line) for k in range(4)]
                groups.append([((x * 2 + w) * 4 + y) * 2 + c for x, y in places])
    return groups


FAR = rings(False)
NEAR = [
    [i ^ flip for i in group for flip in (0, 8)] for group in rings(True) if not group[0] & 8
]
FLIP_C = [(i, i ^ 1) for i in range(64)]


def swap(value, pairs):
    return lax.ppermute(value, "dp", pairs)


def send_mp(value, step):
    return lax.ppermute(value, "mp", [(i, (i + step) % 4) for i in range(4)])


def exchange(blocks, groups):
    return lax.all_to_all(blocks, "dp", 0, 0, axis_index_groups=groups)


def spread(block, copies):
    return jnp.broadcast_to(block[None], (copies, *block.shape))


def attention_probs(query3, key3, doc_ids):
    seq = query3.shape[0]
    scale = 1.0 / math.sqrt(HD)
    scores = jnp.einsum("thd,shd->hts", query3, key3, preferred_element_type=F32) * scale
    pos = lax.iota(jnp.int32, seq)
    allowed = (pos[None, :] <= pos[:, None]) & (doc_ids[None, :] == doc_ids[:, None])
    scores = jnp.where(allowed[None], scores, -1e30)
    top = jnp.max(scores, axis=2, keepdims=True)
    weights = jnp.exp(scores - top)
    return weights / jnp.sum(weights, axis=2, keepdims=True)


def turn_tokens(pos, att_ref, att_s):
    rows = att_ref.shape[0] // 4
    for k in range(4):
        start = pl.multiple_of(((pos[1] + k) % 4) * rows, 16)
        att_s[pl.ds(k * rows, rows), :] = att_ref[pl.ds(start, rows), :]


def place(c, x, y):
    return jnp.where(c == 0, x, y), jnp.where(c == 0, y, x)


def assemble(c, mine, other, w_s):
    piece = mine[0].shape[3]
    for w in range(2):
        for y in range(4):
            i = 2 * (w * 4 + y)
            w_s[pl.ds(pl.multiple_of((i + c) * piece, 16), piece), :] = mine[y][0, 0, w]
            w_s[pl.ds(pl.multiple_of((i + 1 - c) * piece, 16), piece), :] = other[y][0, 0, w]


def weight_specs(piece, width):
    def block(flip, y):
        def at(i, pos):
            return *place(pos[0] ^ flip, i, y), 0, 0, 0

        return pl.BlockSpec((1, 1, 2, piece, width), at)

    return [block(flip, y) for flip in range(2) for y in range(4)]


def branch_kernel(pos, att_ref, *refs):
    p0, p1a, p1b, p2a, p2b, p3a, p3b, att_s, w_s = refs[8:]
    rows = att_ref.shape[0] // 4
    half = rows // 2

    @pl.when(pl.program_id(0) == 0)
    def _():
        turn_tokens(pos, att_ref, att_s)

    assemble(pos[0], refs[:4], refs[4:8], w_s)
    prod = lax.dot_general(
        att_s[...], w_s[...], (((1,), (1,)), ((), ())), preferred_element_type=F32
    ).astype(BF)
    p0[...] = prod[:rows]
    p1a[...] = prod[rows : rows + half]
    p1b[...] = prod[rows + half : 2 * rows]
    p2a[...] = prod[2 * rows : 2 * rows + half]
    p2b[...] = prod[2 * rows + half : 3 * rows]
    p3a[...] = prod[3 * rows : 3 * rows + half]
    p3b[...] = prod[3 * rows + half :]


def branch_part(pos, attended, cat, oth):
    piece, width = cat.shape[3:]
    seq = attended.shape[0]
    rows, span = seq // 4, 16 * piece
    total = 4 * span
    heights = (rows,) + (rows // 2,) * 6
    return pl.pallas_call(
        branch_kernel,
        grid_spec=pltpu.PrefetchScalarGridSpec(
            num_scalar_prefetch=1,
            grid=(4,),
            in_specs=[pl.BlockSpec((seq, width), lambda i, pos: (0, 0))]
            + weight_specs(piece, width),
            out_specs=[pl.BlockSpec((h, span), lambda i, pos: (0, i)) for h in heights],
            scratch_shapes=[pltpu.VMEM((seq, width), BF), pltpu.VMEM((span, width), BF)],
        ),
        out_shape=[jax.ShapeDtypeStruct((h, total), BF) for h in heights],
        compiler_params=pltpu.CompilerParams(vmem_limit_bytes=VMEM_LIMIT),
        cost_estimate=pl.CostEstimate(
            flops=2 * seq * width * total,
            bytes_accessed=2 * (total * width + seq * total),
            transcendentals=0,
        ),
        name="branch_part",
    )(pos, attended, *[cat] * 4, *[oth] * 4)


def gather_rows(g0, gp, ga, gb, gm, rows_s):
    rows = g0.shape[0]
    half = rows // 2
    rows_s[pl.ds(0, rows), :] = g0[...]
    rows_s[pl.ds(rows, rows), :] = gp[...]
    rows_s[pl.ds(2 * rows, half), :] = ga[...]
    rows_s[pl.ds(2 * rows + half, half), :] = gb[...]
    rows_s[pl.ds(3 * rows, rows), :] = gm[...]


def weight_kernel(pos, g0, gp, ga, gb, gm, att_ref, keep, send, att_s, rows_s):
    piece = keep.shape[3]
    c = pos[0]
    step = pl.program_id(0)

    @pl.when(step == 0)
    def _():
        turn_tokens(pos, att_ref, att_s)

    gather_rows(g0, gp, ga, gb, gm, rows_s)
    prod = lax.dot_general(
        rows_s[...], att_s[...], (((0,), (0,)), ((), ())), preferred_element_type=F32
    ).astype(BF)
    for w in range(2):
        for y in range(4):
            i = 2 * (w * 4 + y)
            even = prod[i * piece : (i + 1) * piece]
            odd = prod[(i + 1) * piece : (i + 2) * piece]
            far, near = place(c, step, y)
            keep[far, near, w] = jnp.where(c == 0, even, odd)
            send[near, far, w] = jnp.where(c == 0, odd, even)


def weight_part(pos, parts, attended, piece):
    seq, width = attended.shape
    span = 16 * piece
    shape = (4, 4, 2, piece, width)
    block = pl.BlockSpec(memory_space=pltpu.VMEM)
    return pl.pallas_call(
        weight_kernel,
        grid=(4,),
        in_specs=[pl.BlockSpec(memory_space=pltpu.SMEM)]
        + [pl.BlockSpec((g.shape[0], span), lambda i: (0, i)) for g in parts]
        + [pl.BlockSpec((seq, width), lambda i: (0, 0))],
        out_specs=[block, block],
        out_shape=[jax.ShapeDtypeStruct(shape, BF)] * 2,
        scratch_shapes=[pltpu.VMEM((seq, width), BF), pltpu.VMEM((seq, span), BF)],
        compiler_params=pltpu.CompilerParams(vmem_limit_bytes=VMEM_LIMIT),
        cost_estimate=pl.CostEstimate(
            flops=8 * seq * width * span,
            bytes_accessed=8 * (span * width + seq * span),
            transcendentals=0,
        ),
        name="weight_part",
    )(pos, *parts, attended)


def attended_kernel(pos, g0, gp, ga, gb, gm, *refs):
    out_ref, rows_s, w_s, acc = refs[8:]
    m = pos[1]
    rows = g0.shape[0]
    step = pl.program_id(0)

    @pl.when(step == 0)
    def _():
        acc[...] = jnp.zeros_like(acc)

    gather_rows(g0, gp, ga, gb, gm, rows_s)
    assemble(pos[0], refs[:4], refs[4:8], w_s)
    acc[...] += jnp.dot(rows_s[...], w_s[...], preferred_element_type=F32)

    @pl.when(step == pl.num_programs(0) - 1)
    def _():
        for k in range(4):
            start = pl.multiple_of(((m + k) % 4) * rows, 16)
            out_ref[pl.ds(start, rows), :] = acc[pl.ds(k * rows, rows), :].astype(BF)


def attended_part(pos, parts, cat, oth):
    piece, width = cat.shape[3:]
    seq = 4 * parts[0].shape[0]
    span = 16 * piece
    return pl.pallas_call(
        attended_kernel,
        grid_spec=pltpu.PrefetchScalarGridSpec(
            num_scalar_prefetch=1,
            grid=(4,),
            in_specs=[pl.BlockSpec((g.shape[0], span), lambda i, pos: (0, i)) for g in parts]
            + weight_specs(piece, width),
            out_specs=pl.BlockSpec((seq, width), lambda i, pos: (0, 0)),
            scratch_shapes=[
                pltpu.VMEM((seq, span), BF),
                pltpu.VMEM((span, width), BF),
                pltpu.VMEM((seq, width), F32),
            ],
        ),
        out_shape=jax.ShapeDtypeStruct((seq, width), BF),
        compiler_params=pltpu.CompilerParams(vmem_limit_bytes=VMEM_LIMIT),
        cost_estimate=pl.CostEstimate(
            flops=8 * seq * width * span,
            bytes_accessed=8 * (span * width + seq * span),
            transcendentals=0,
        ),
        name="attended_part",
    )(pos, *parts, *[cat] * 4, *[oth] * 4)


def sum_kernel(in_ref, out_ref):
    total = in_ref[0].astype(F32)
    for k in range(1, 4):
        total = total + in_ref[k].astype(F32)
    out_ref[...] = total.astype(BF)


def sum_blocks(blocks):
    piece, width = blocks.shape[3:]
    return pl.pallas_call(
        sum_kernel,
        grid=(4,),
        in_specs=[pl.BlockSpec((4, 1, 2, piece, width), lambda i: (0, i, 0, 0, 0))],
        out_specs=pl.BlockSpec((1, 2, piece, width), lambda i: (i, 0, 0, 0)),
        out_shape=jax.ShapeDtypeStruct((4, 2, piece, width), BF),
        compiler_params=pltpu.CompilerParams(vmem_limit_bytes=VMEM_LIMIT),
        cost_estimate=pl.CostEstimate(
            flops=32 * piece * width, bytes_accessed=80 * piece * width, transcendentals=0
        ),
        name="sum_blocks",
    )(blocks)


def sum_f32(*parts):
    total = parts[0].astype(F32)
    for part in parts[1:]:
        total = total + part.astype(F32)
    return total


def on_device(query, key, value, residual, cotangent, out_weight, norm_gain, doc_ids):
    seq, width = query.shape
    heads = width // HD
    piece = out_weight.shape[0]
    rows, d_model = residual.shape
    half = rows // 2
    scale = 1.0 / math.sqrt(HD)
    dp = lax.axis_index("dp")
    c = dp % 2
    m = lax.axis_index("mp")
    pos = jnp.stack([c, m]).astype(jnp.int32)

    planes = exchange(spread(out_weight, 8), NEAR).reshape(4, 2, piece, width)
    cat = exchange(spread(planes, 4), FAR)

    query3 = query.reshape(seq, heads, HD)
    key3 = key.reshape(seq, heads, HD)
    value3 = value.reshape(seq, heads, HD)
    probs = attention_probs(query3, key3, doc_ids)
    probs_b = probs.astype(BF)
    attended = jnp.einsum("hts,shd->thd", probs_b, value3, preferred_element_type=F32)
    attended = attended.astype(BF).reshape(seq, width)

    cat, attended = lax.optimization_barrier((cat, attended))
    oth = swap(cat, FLIP_C)
    p0, p1a, p1b, p2a, p2b, p3a, p3b = branch_part(pos, attended, cat, oth)
    ra, rb = send_mp(p2a, 1), send_mp(p2b, -1)
    up_b, down_a = send_mp(p1b, 1), send_mp(p3a, -1)
    up_a = send_mp(sum_f32(p1a, ra).astype(BF), 1)
    down_b = send_mp(sum_f32(p3b, rb).astype(BF), -1)
    up = jnp.concatenate([up_a, up_b])
    down = jnp.concatenate([down_a, down_b])
    mixed = sum_f32(residual, p0, up, down)
    cot = cotangent.astype(F32)
    gscaled = cot * norm_gain
    inv = lax.rsqrt(jnp.mean(mixed * mixed, axis=1, keepdims=True) + 1e-05)
    mean_dot = jnp.mean(gscaled * mixed, axis=1, keepdims=True)
    grad_residual = (inv * (gscaled - mixed * inv * inv * mean_dot)).astype(BF)

    tie = lax.optimization_barrier

    def add_from(total, bits):
        for bit in bits:
            total = total + swap(total, [(i, i ^ bit) for i in range(64)])
        return total

    gain = jnp.sum(cot * mixed * inv, axis=0).reshape(d_model // 128, 128)
    gm = send_mp(grad_residual, 1)
    gp = send_mp(grad_residual, -1)
    gm, gp, gain = tie((gm, gp, add_from(gain, (2, 4, 16, 32))))
    ga = send_mp(gm[:half], 1)
    gb = send_mp(gp[half:], -1)
    parts = (grad_residual, gp, ga, gb, gm)
    keep, send = weight_part(pos, parts, attended, piece)
    swapped, grad_attended = tie((swap(send, FLIP_C), attended_part(pos, parts, cat, oth)))
    both = sum_f32(keep, swapped).astype(BF)
    part = exchange(both, FAR)
    gain = add_from(gain, (1, 8))
    for bit in (1, 2):
        gain = gain + lax.ppermute(gain, "mp", [(i, i ^ bit) for i in range(4)])
    part, gain = tie((part, gain))
    part = sum_blocks(part).reshape(8, piece, width)
    grad_weight = sum_f32(*exchange(part, NEAR)) / 64
    grad_gain = lax.dynamic_slice_in_dim(gain.reshape(d_model) / 64, dp * piece, piece, 0)

    grad3 = grad_attended.reshape(seq, heads, HD)
    grad_value = jnp.einsum("hts,thd->shd", probs_b, grad3, preferred_element_type=F32)
    grad_value = grad_value.astype(BF).reshape(seq, width)
    grad_probs = jnp.einsum("thd,shd->hts", grad3, value3, preferred_element_type=F32)
    delta = jnp.sum(probs * grad_probs, axis=2, keepdims=True)
    grad_scores = (probs * (grad_probs - delta)).astype(BF)
    grad_query = jnp.einsum("hts,shd->thd", grad_scores, key3, preferred_element_type=F32) * scale
    grad_key = jnp.einsum("hts,thd->shd", grad_scores, query3, preferred_element_type=F32) * scale
    grad_query = grad_query.astype(BF).reshape(seq, width)
    grad_key = grad_key.astype(BF).reshape(seq, width)
    return (grad_query, grad_key, grad_value, grad_residual, grad_weight, grad_gain)


def solution(mesh):
    placed = (
        P("dp", "mp"),
        P("dp", "mp"),
        P("dp", "mp"),
        P(("dp", "mp"), None),
        P(("dp", "mp"), None),
        P("dp", "mp"),
        P(),
        P("dp"),
    )
    return jax.shard_map(
        on_device,
        mesh=mesh,
        in_specs=placed,
        out_specs=(
            P("dp", "mp"),
            P("dp", "mp"),
            P("dp", "mp"),
            P(("dp", "mp"), None),
            P("dp", "mp"),
            P("dp"),
        ),
        check_vma=False,
    )
```

```python
import math

import jax
import jax.numpy as jnp
from jax import lax
from jax.experimental import pallas as pl
from jax.experimental.pallas import tpu as pltpu
from jax.sharding import PartitionSpec as P

HD = 128
BF = jnp.bfloat16
F32 = jnp.float32
VMEM_LIMIT = 40 * 1024 * 1024


def rings(along_y):
    groups = []
    for c in range(2):
        for w in range(2):
            for line in range(4):
                places = [(line, k) if (c == 0) == along_y else (k, line) for k in range(4)]
                groups.append([((x * 2 + w) * 4 + y) * 2 + c for x, y in places])
    return groups


FAR = rings(False)
NEAR = [
    [i ^ flip for i in group for flip in (0, 8)] for group in rings(True) if not group[0] & 8
]
FLIP_C = [(i, i ^ 1) for i in range(64)]


def swap(value, pairs):
    return lax.ppermute(value, "dp", pairs)


def send_mp(value, step):
    return lax.ppermute(value, "mp", [(i, (i + step) % 4) for i in range(4)])


def exchange(blocks, groups):
    return lax.all_to_all(blocks, "dp", 0, 0, axis_index_groups=groups)


def spread(block, copies):
    return jnp.broadcast_to(block[None], (copies, *block.shape))


def attention_probs(query3, key3, doc_ids):
    seq = query3.shape[0]
    scale = 1.0 / math.sqrt(HD)
    scores = jnp.einsum("thd,shd->hts", query3, key3, preferred_element_type=F32) * scale
    pos = lax.iota(jnp.int32, seq)
    allowed = (pos[None, :] <= pos[:, None]) & (doc_ids[None, :] == doc_ids[:, None])
    scores = jnp.where(allowed[None], scores, -1e30)
    top = jnp.max(scores, axis=2, keepdims=True)
    weights = jnp.exp(scores - top)
    return weights / jnp.sum(weights, axis=2, keepdims=True)


def turn_tokens(pos, att_ref, att_s):
    rows = att_ref.shape[0] // 4
    for k in range(4):
        start = pl.multiple_of(((pos[1] + k) % 4) * rows, 16)
        att_s[pl.ds(k * rows, rows), :] = att_ref[pl.ds(start, rows), :]


def place(c, x, y):
    return jnp.where(c == 0, x, y), jnp.where(c == 0, y, x)


def assemble(c, mine, other, w_s):
    piece = mine[0].shape[3]
    for w in range(2):
        for y in range(4):
            i = 2 * (w * 4 + y)
            w_s[pl.ds(pl.multiple_of((i + c) * piece, 16), piece), :] = mine[y][0, 0, w]
            w_s[pl.ds(pl.multiple_of((i + 1 - c) * piece, 16), piece), :] = other[y][0, 0, w]


def weight_specs(piece, width):
    def block(flip, y):
        def at(i, pos):
            return *place(pos[0] ^ flip, i, y), 0, 0, 0

        return pl.BlockSpec((1, 1, 2, piece, width), at)

    return [block(flip, y) for flip in range(2) for y in range(4)]


def branch_kernel(pos, att_ref, *refs):
    p0, p1a, p1b, p2a, p2b, p3a, p3b, att_s, w_s = refs[8:]
    rows = att_ref.shape[0] // 4
    half = rows // 2

    @pl.when(pl.program_id(0) == 0)
    def _():
        turn_tokens(pos, att_ref, att_s)

    assemble(pos[0], refs[:4], refs[4:8], w_s)
    prod = lax.dot_general(
        att_s[...], w_s[...], (((1,), (1,)), ((), ())), preferred_element_type=F32
    ).astype(BF)
    p0[...] = prod[:rows]
    p1a[...] = prod[rows : rows + half]
    p1b[...] = prod[rows + half : 2 * rows]
    p2a[...] = prod[2 * rows : 2 * rows + half]
    p2b[...] = prod[2 * rows + half : 3 * rows]
    p3a[...] = prod[3 * rows : 3 * rows + half]
    p3b[...] = prod[3 * rows + half :]


def branch_part(pos, attended, cat, oth):
    piece, width = cat.shape[3:]
    seq = attended.shape[0]
    rows, span = seq // 4, 16 * piece
    total = 4 * span
    heights = (rows,) + (rows // 2,) * 6
    return pl.pallas_call(
        branch_kernel,
        grid_spec=pltpu.PrefetchScalarGridSpec(
            num_scalar_prefetch=1,
            grid=(4,),
            in_specs=[pl.BlockSpec((seq, width), lambda i, pos: (0, 0))]
            + weight_specs(piece, width),
            out_specs=[pl.BlockSpec((h, span), lambda i, pos: (0, i)) for h in heights],
            scratch_shapes=[pltpu.VMEM((seq, width), BF), pltpu.VMEM((span, width), BF)],
        ),
        out_shape=[jax.ShapeDtypeStruct((h, total), BF) for h in heights],
        compiler_params=pltpu.CompilerParams(vmem_limit_bytes=VMEM_LIMIT),
        cost_estimate=pl.CostEstimate(
            flops=2 * seq * width * total,
            bytes_accessed=2 * (total * width + seq * total),
            transcendentals=0,
        ),
        name="branch_part",
    )(pos, attended, *[cat] * 4, *[oth] * 4)


def gather_rows(parts, rows_s):
    start = 0
    for part in parts:
        rows_s[pl.ds(start, part.shape[0]), :] = part[...]
        start += part.shape[0]


def weight_kernel(pos, *refs):
    parts, (att_ref, keep, send, att_s, rows_s) = refs[:7], refs[7:]
    piece = keep.shape[3]
    c = pos[0]
    step = pl.program_id(0)

    @pl.when(step == 0)
    def _():
        turn_tokens(pos, att_ref, att_s)

    gather_rows(parts, rows_s)
    prod = lax.dot_general(
        rows_s[...], att_s[...], (((0,), (0,)), ((), ())), preferred_element_type=F32
    ).astype(BF)
    for w in range(2):
        for y in range(4):
            i = 2 * (w * 4 + y)
            even = prod[i * piece : (i + 1) * piece]
            odd = prod[(i + 1) * piece : (i + 2) * piece]
            far, near = place(c, step, y)
            keep[far, near, w] = jnp.where(c == 0, even, odd)
            send[near, far, w] = jnp.where(c == 0, odd, even)


def weight_part(pos, parts, attended, piece):
    seq, width = attended.shape
    span = 16 * piece
    shape = (4, 4, 2, piece, width)
    block = pl.BlockSpec(memory_space=pltpu.VMEM)
    return pl.pallas_call(
        weight_kernel,
        grid=(4,),
        in_specs=[pl.BlockSpec(memory_space=pltpu.SMEM)]
        + [pl.BlockSpec((g.shape[0], span), lambda i: (0, i)) for g in parts]
        + [pl.BlockSpec((seq, width), lambda i: (0, 0))],
        out_specs=[block, block],
        out_shape=[jax.ShapeDtypeStruct(shape, BF)] * 2,
        scratch_shapes=[pltpu.VMEM((seq, width), BF), pltpu.VMEM((seq, span), BF)],
        compiler_params=pltpu.CompilerParams(vmem_limit_bytes=VMEM_LIMIT),
        cost_estimate=pl.CostEstimate(
            flops=8 * seq * width * span,
            bytes_accessed=8 * (span * width + seq * span),
            transcendentals=0,
        ),
        name="weight_part",
    )(pos, *parts, attended)


def attended_kernel(pos, *refs):
    parts, refs = refs[:7], refs[7:]
    out_ref, rows_s, w_s, acc = refs[8:]
    m = pos[1]
    rows = parts[0].shape[0]
    step = pl.program_id(0)

    @pl.when(step == 0)
    def _():
        acc[...] = jnp.zeros_like(acc)

    gather_rows(parts, rows_s)
    assemble(pos[0], refs[:4], refs[4:8], w_s)
    acc[...] += jnp.dot(rows_s[...], w_s[...], preferred_element_type=F32)

    @pl.when(step == pl.num_programs(0) - 1)
    def _():
        for k in range(4):
            start = pl.multiple_of(((m + k) % 4) * rows, 16)
            out_ref[pl.ds(start, rows), :] = acc[pl.ds(k * rows, rows), :].astype(BF)


def attended_part(pos, parts, cat, oth):
    piece, width = cat.shape[3:]
    seq = 4 * parts[0].shape[0]
    span = 16 * piece
    return pl.pallas_call(
        attended_kernel,
        grid_spec=pltpu.PrefetchScalarGridSpec(
            num_scalar_prefetch=1,
            grid=(4,),
            in_specs=[pl.BlockSpec((g.shape[0], span), lambda i, pos: (0, i)) for g in parts]
            + weight_specs(piece, width),
            out_specs=pl.BlockSpec((seq, width), lambda i, pos: (0, 0)),
            scratch_shapes=[
                pltpu.VMEM((seq, span), BF),
                pltpu.VMEM((span, width), BF),
                pltpu.VMEM((seq, width), F32),
            ],
        ),
        out_shape=jax.ShapeDtypeStruct((seq, width), BF),
        compiler_params=pltpu.CompilerParams(vmem_limit_bytes=VMEM_LIMIT),
        cost_estimate=pl.CostEstimate(
            flops=8 * seq * width * span,
            bytes_accessed=8 * (span * width + seq * span),
            transcendentals=0,
        ),
        name="attended_part",
    )(pos, *parts, *[cat] * 4, *[oth] * 4)


def sum_kernel(in_ref, out_ref):
    total = in_ref[0].astype(F32)
    for k in range(1, 4):
        total = total + in_ref[k].astype(F32)
    out_ref[...] = total.astype(BF)


def sum_blocks(blocks):
    piece, width = blocks.shape[3:]
    return pl.pallas_call(
        sum_kernel,
        grid=(4,),
        in_specs=[pl.BlockSpec((4, 1, 2, piece, width), lambda i: (0, i, 0, 0, 0))],
        out_specs=pl.BlockSpec((1, 2, piece, width), lambda i: (i, 0, 0, 0)),
        out_shape=jax.ShapeDtypeStruct((4, 2, piece, width), BF),
        compiler_params=pltpu.CompilerParams(vmem_limit_bytes=VMEM_LIMIT),
        cost_estimate=pl.CostEstimate(
            flops=32 * piece * width, bytes_accessed=80 * piece * width, transcendentals=0
        ),
        name="sum_blocks",
    )(blocks)


def sum_f32(*parts):
    total = parts[0].astype(F32)
    for part in parts[1:]:
        total = total + part.astype(F32)
    return total


def on_device(query, key, value, residual, cotangent, out_weight, norm_gain, doc_ids):
    seq, width = query.shape
    heads = width // HD
    piece = out_weight.shape[0]
    rows, d_model = residual.shape
    half = rows // 2
    scale = 1.0 / math.sqrt(HD)
    dp = lax.axis_index("dp")
    c = dp % 2
    m = lax.axis_index("mp")
    pos = jnp.stack([c, m]).astype(jnp.int32)

    planes = exchange(spread(out_weight, 8), NEAR).reshape(4, 2, piece, width)
    cat = exchange(spread(planes, 4), FAR)

    query3 = query.reshape(seq, heads, HD)
    key3 = key.reshape(seq, heads, HD)
    value3 = value.reshape(seq, heads, HD)
    probs = attention_probs(query3, key3, doc_ids)
    probs_b = probs.astype(BF)
    attended = jnp.einsum("hts,shd->thd", probs_b, value3, preferred_element_type=F32)
    attended = attended.astype(BF).reshape(seq, width)

    cat, attended = lax.optimization_barrier((cat, attended))
    oth = swap(cat, FLIP_C)
    p0, p1a, p1b, p2a, p2b, p3a, p3b = branch_part(pos, attended, cat, oth)
    ra, rb = send_mp(p2a, 1), send_mp(p2b, -1)
    up_b, down_a = send_mp(p1b, 1), send_mp(p3a, -1)
    up_a = send_mp(sum_f32(p1a, ra).astype(BF), 1)
    down_b = send_mp(sum_f32(p3b, rb).astype(BF), -1)
    up = jnp.concatenate([up_a, up_b])
    down = jnp.concatenate([down_a, down_b])
    mixed = sum_f32(residual, p0, up, down)
    cot = cotangent.astype(F32)
    gscaled = cot * norm_gain
    inv = lax.rsqrt(jnp.mean(mixed * mixed, axis=1, keepdims=True) + 1e-05)
    mean_dot = jnp.mean(gscaled * mixed, axis=1, keepdims=True)
    grad_residual = (inv * (gscaled - mixed * inv * inv * mean_dot)).astype(BF)

    tie = lax.optimization_barrier

    def add_from(total, bits):
        for bit in bits:
            total = total + swap(total, [(i, i ^ bit) for i in range(64)])
        return total

    gain = jnp.sum(cot * mixed * inv, axis=0).reshape(d_model // 128, 128)
    low, high = grad_residual[:half], grad_residual[half:]
    gma, gpb = send_mp(low, 1), send_mp(high, -1)
    gmb, gpa = send_mp(high, 1), send_mp(low, -1)
    gma, gpb, gain = tie((gma, gpb, add_from(gain, (2, 4))))
    ga, gb = send_mp(gma, 1), send_mp(gpb, -1)
    gmb, gpa, gain = tie((gmb, gpa, add_from(gain, (16, 32))))
    parts = (grad_residual, gpa, gpb, ga, gb, gma, gmb)
    keep, send = weight_part(pos, parts, attended, piece)
    swapped, grad_attended = tie((swap(send, FLIP_C), attended_part(pos, parts, cat, oth)))
    both = sum_f32(keep, swapped).astype(BF)
    part = exchange(both, FAR)
    gain = add_from(gain, (1, 8))
    for bit in (1, 2):
        gain = gain + lax.ppermute(gain, "mp", [(i, i ^ bit) for i in range(4)])
    part, gain = tie((part, gain))
    part = sum_blocks(part).reshape(8, piece, width)
    grad_weight = sum_f32(*exchange(part, NEAR)) / 64
    grad_gain = lax.dynamic_slice_in_dim(gain.reshape(d_model) / 64, dp * piece, piece, 0)

    grad3 = grad_attended.reshape(seq, heads, HD)
    grad_value = jnp.einsum("hts,thd->shd", probs_b, grad3, preferred_element_type=F32)
    grad_value = grad_value.astype(BF).reshape(seq, width)
    grad_probs = jnp.einsum("thd,shd->hts", grad3, value3, preferred_element_type=F32)
    delta = jnp.sum(probs * grad_probs, axis=2, keepdims=True)
    grad_scores = (probs * (grad_probs - delta)).astype(BF)
    grad_query = jnp.einsum("hts,shd->thd", grad_scores, key3, preferred_element_type=F32) * scale
    grad_key = jnp.einsum("hts,thd->shd", grad_scores, query3, preferred_element_type=F32) * scale
    grad_query = grad_query.astype(BF).reshape(seq, width)
    grad_key = grad_key.astype(BF).reshape(seq, width)
    return (grad_query, grad_key, grad_value, grad_residual, grad_weight, grad_gain)


def solution(mesh):
    placed = (
        P("dp", "mp"),
        P("dp", "mp"),
        P("dp", "mp"),
        P(("dp", "mp"), None),
        P(("dp", "mp"), None),
        P("dp", "mp"),
        P(),
        P("dp"),
    )
    return jax.shard_map(
        on_device,
        mesh=mesh,
        in_specs=placed,
        out_specs=(
            P("dp", "mp"),
            P("dp", "mp"),
            P("dp", "mp"),
            P(("dp", "mp"), None),
            P("dp", "mp"),
            P("dp"),
        ),
        check_vma=False,
    )
```
